256 devices in a mesh: row: 32 (over x, z_lo, core), col: 8 (over z_hi, y).
Axes of the slice: x: 4, y: 4, z: 8 (z_hi: 2, z_lo: 4; z = z_hi * 4 + z_lo), core: 2. Of those that a mesh axis runs over, the one named last changes fastest.
Arguments:
- s_band: bfloat16 [256, 65536], P(None, ('col', 'row')), may hold values from -6 to 6
- t_band: bfloat16 [256, 65536], P(None, ('col', 'row')), may hold values from -6 to 6
- q_rows: bfloat16 [4096, 65536], P('row', 'col'), may hold values from -6 to 6
- z_rows: bfloat16 [4096, 65536], P('row', 'col'), may hold values from -6 to 6
- factors: bfloat16 [16, 2, 256, 256], P(None, None, 'row', 'col'), may hold values from -0.375 to 0.375
- starts: int32 [16], replicated, may hold values from 0 to 65280, as said below
- flags: int32 [16], replicated, may hold values from 0 to 1, as said below
Outputs:
- q_out: bfloat16 [4096, 65536], P('row', 'col')
- z_out: bfloat16 [4096, 65536], P('row', 'col')
- s_out: bfloat16 [256, 65536], P(None, ('col', 'row'))
- t_out: bfloat16 [256, 65536], P(None, ('col', 'row'))
The draws below stay inside these ranges and needn't reach their ends.
Inputs may be any that keep to these rules, and one draw needn't show every extreme that they name: The starts are distinct multiples of 256; starts[0] = 0. At most 8 windows start within the columns of one index of col, and exactly 8 do for some index. flags[0] = 1.
All inputs are finite; a program needn't handle non-finite values.
Results may differ from the reference program's by a relative error of at most 0.0013.
Values may be sent and summed in bfloat16 or wider, within the bound.
A program may use at most 64 MiB of HBM per device.

```python
import jax
import jax.numpy as jnp
from jax import lax

N = 65536
W = 256
K = 16
MOST = 8
QROWS = 4096
TILE_GROUP = 32


def draw_starts(key, part):
    key_group = jax.random.fold_in(key, 11)
    key_score = jax.random.fold_in(key, 12)
    n_tiles = N // W
    tile = jnp.arange(n_tiles, dtype=jnp.int32)
    group = tile // TILE_GROUP
    n_groups = n_tiles // TILE_GROUP
    chosen_group = jax.random.randint(key_group, (), 0, n_groups, dtype=jnp.int32)
    score = jax.random.randint(key_score, (n_tiles,), 0, 4096, dtype=jnp.int32) * n_tiles + tile
    forced = (tile == 0) | (tile == n_tiles - 1)
    inside = (group == chosen_group) & ~forced
    _, group_pick = lax.top_k(jnp.where(inside, score, -1), MOST)
    needed = MOST - (chosen_group == 0).astype(jnp.int32) - (chosen_group == n_groups - 1).astype(jnp.int32)
    marked = jnp.zeros((n_tiles,), jnp.int32).at[group_pick].set((jnp.arange(MOST, dtype=jnp.int32) < needed).astype(jnp.int32))
    others = (group != chosen_group) & ~forced
    tier = jnp.where(forced, 3, jnp.where(marked == 1, 2, jnp.where(others, 1, 0)))
    final = tier * (4096 * n_tiles) + score
    _, picked = lax.top_k(final, K)
    ordered = jnp.where(picked == 0, -1, picked)
    arranged = jnp.sort(ordered)
    result = jnp.where(arranged < 0, 0, arranged)
    return (result * W).astype(jnp.int32)


def draw_flags(key, part):
    values = jax.random.randint(jax.random.fold_in(key, 21), (K,), 0, 4, dtype=jnp.int32)
    marks = (values > 0).astype(jnp.int32)
    return marks.at[0].set(1)


def levels(own_key, dims, shards, least, high):
    def one(dim, shards_of):
        heights = jax.random.uniform(jax.random.fold_in(jax.random.fold_in(own_key, 6), dim), (shards_of,), jnp.float32, least / len(shards), high / len(shards))
        return jnp.repeat(jnp.exp(heights), dims[dim] // shards_of).reshape((-1,) + (1,) * (len(dims) - dim - 1))

    gain = one(*shards[0])
    for cut in shards[1:]:
        gain = gain * one(*cut)
    return gain


def centred(own_key, shape, spread, most, pieces=(), kind=jnp.bfloat16):
    level = levels(own_key, shape, pieces, -0.22, 0.18) if pieces else 1.0
    values = jax.random.normal(own_key, shape, jnp.float32) * spread * level
    return jnp.minimum(jnp.maximum(values, -most), most).astype(kind)


def setup_inputs(seed: int = 0) -> dict:
    arg_keys = jax.random.split(jax.random.key(seed), 8)
    return {
        "s_band": centred(arg_keys[0], (W, N), 1.0, 6.0, ((1, 256),)),
        "t_band": centred(arg_keys[1], (W, N), 1.0, 6.0, ((1, 256),)),
        "q_rows": centred(arg_keys[2], (QROWS, N), 1.0, 6.0, ((0, 32), (1, 8))),
        "z_rows": centred(arg_keys[3], (QROWS, N), 1.0, 6.0, ((0, 32), (1, 8))),
        "factors": centred(arg_keys[4], (K, 2, W, W), W ** -0.5, 0.375, ((2, 32), (3, 8))),
        "starts": draw_starts(jax.random.fold_in(arg_keys[7], 71), 0),
        "flags": draw_flags(jax.random.fold_in(arg_keys[7], 71), 0),
    }


def update_columns(matrix, place, factor, active):
    block = lax.dynamic_slice_in_dim(matrix, place, W, 1)
    fresh = jnp.dot(block, factor, preferred_element_type=jnp.float32).astype(matrix.dtype)
    value = jnp.where(active, fresh, block)
    return lax.dynamic_update_slice_in_dim(matrix, value, place, 1)


def reference(s_band, t_band, q_rows, z_rows, factors, starts, flags):
    def apply_window(index, carry):
        q_now, z_now, s_now, t_now = carry
        place = starts[index].astype(jnp.int32)
        active = flags[index] == 1
        left = factors[index, 0]
        right = factors[index, 1]
        q_now = update_columns(q_now, place, left, active)
        z_now = update_columns(z_now, place, right, active)
        s_now = update_columns(s_now, place, right, active)
        t_now = update_columns(t_now, place, right, active)
        return (q_now, z_now, s_now, t_now)

    q_out, z_out, s_mid, t_mid = lax.fori_loop(0, K, apply_window, (q_rows, z_rows, s_band, t_band))
    lead = factors[0, 0]
    s_out = lax.dot_general(lead, s_mid, (((0,), (0,)), ((), ())), preferred_element_type=jnp.float32).astype(s_band.dtype)
    t_out = lax.dot_general(lead, t_mid, (((0,), (0,)), ((), ())), preferred_element_type=jnp.float32).astype(t_band.dtype)
    return (q_out, z_out, s_out, t_out)
```

```python
import jax
import jax.numpy as jnp
from jax import lax
from jax.experimental import pallas as pl
from jax.experimental.pallas import tpu as pltpu
from jax.sharding import PartitionSpec as P

W = 256
K = 16
SLOTS = 8
UNITS = 2 * SLOTS + 1
ROWS = 32
COLS = 8
TILES = 32
HALF = 9
BF = jnp.bfloat16
F32 = jnp.float32


def slot_words(starts_ref, column):
    word = jnp.int32(0)
    for k in reversed(range(K)):
        mine = (starts_ref[k] >> 13) == column
        word = jnp.where(mine, (word << 4) | k, word)
    return word


def remote(src, dst, send_sem, recv_sem, device):
    return pltpu.make_async_remote_copy(
        src_ref=src,
        dst_ref=dst,
        send_sem=send_sem,
        recv_sem=recv_sem,
        device_id=device,
        device_id_type=pl.DeviceIdType.MESH,
    )


def gather_kernel(
    starts_hbm, factors_hbm, q_hbm, z_hbm, s_hbm, t_hbm,
    g_ref, qv, zv, sv, tv,
    starts_ref, fac, wide, send1, recv1, send0, recv0,
    load_sem, ss1, rs1, ss0, rs0, sz, rz, sxp, rxp, sxm, rxm, sop, rop, som, rom, ssib, rsib,
):
    r = lax.axis_index("row")
    c = lax.axis_index("col")
    core = r % 2
    x = r // 8
    zl = (r // 2) % 4
    me = core * 8 + c
    xp = (r + 8) % ROWS
    xm = (r + ROWS - 8) % ROWS
    sib = r + 1 - 2 * core
    base = r - core

    barrier = pltpu.get_barrier_semaphore()

    def greet(device):
        pl.semaphore_signal(barrier, inc=1, device_id=device, device_id_type=pl.DeviceIdType.MESH)

    loads = [
        pltpu.make_async_copy(a, b, load_sem.at[i])
        for i, (a, b) in enumerate(
            [(factors_hbm, fac), (starts_hbm, starts_ref), (q_hbm, qv), (z_hbm, zv), (s_hbm, sv), (t_hbm, tv)]
        )
    ]
    loads[0].start()
    loads[1].start()
    for k in range(1, 16):
        other = (me + k) % 16
        greet((base + other // 8, other % 8))
    greet((xp, c))
    greet((xm, c))

    @pl.when(zl < 3)
    def _():
        greet((r + 2, c))

    @pl.when(zl > 0)
    def _():
        greet((r - 2, c))

    wide[...] = jnp.zeros_like(wide)
    loads[0].wait()
    loads[1].wait()
    for load in loads[2:]:
        load.start()
    for k in range(K):
        for m in range(2):
            wide[k, 8 * m : 8 * m + 8, 0:32] = fac[k, m].astype(F32)
    for dest in range(COLS):
        word = slot_words(starts_ref, dest)
        rows = []
        for a in range(2):
            total = None
            for b in range(4):
                k = (word >> (4 * (4 * a + b))) & 15
                piece = wide[k]
                if b:
                    piece = pltpu.roll(piece, 32 * b, 1)
                total = piece if total is None else total + piece
            rows.append(total)
        for m in range(2):
            send1[m * 8 + dest] = jnp.concatenate(
                [rows[0][8 * m : 8 * m + 8], rows[1][8 * m : 8 * m + 8]], axis=0
            ).astype(BF)
    lead = wide[0, 0:8]
    placed = lead
    for b in range(1, 4):
        placed = jnp.where(c % 4 == b, pltpu.roll(lead, 32 * b, 1), placed)
    nothing = jnp.zeros_like(placed)
    send0[...] = jnp.concatenate(
        [jnp.where(core == 0, placed, nothing), jnp.where(core == 1, placed, nothing)], axis=0
    ).astype(BF)

    pl.semaphore_wait(
        barrier, 17 + jnp.where(zl < 3, 1, 0) + jnp.where(zl > 0, 1, 0)
    )

    first = []
    for k in range(1, 16):
        other = (me + k) % 16
        copy = remote(send1.at[other], recv1.at[me], ss1.at[k], rs1.at[me], (base + other // 8, other % 8))
        copy.start()
        first.append(copy)
    half = c // 4
    mine0 = core * 4 + c % 4
    lead_copies = []
    for k in range(COLS):
        dest = (c + k) % COLS
        copy = remote(send0, recv0.at[mine0], ss0.at[k], rs0.at[mine0], (base + half, dest))
        if k == 0:
            pl.when(half != core)(copy.start)
        else:
            copy.start()
        lead_copies.append(copy)
    recv1[me] = send1[me]

    @pl.when(half == core)
    def _():
        recv0[mine0] = send0[...]

    for k in range(1, 16):
        other = (me + k) % 16
        remote(recv1.at[other], recv1.at[other], ss1.at[k], rs1.at[other], (sib, c)).wait_recv()
    for k in range(8):
        wait = remote(recv0.at[k], recv0.at[k], ss0.at[0], rs0.at[k], (sib, c)).wait_recv
        pl.when(jnp.logical_or(half != core, k != mine0))(wait)

    lane = lax.broadcasted_iota(jnp.int32, (16, 128), 1) // 32
    for h in range(2):
        turned = {}
        for s in range(2):
            for cc in range(4):
                piece = recv1[s * 8 + 4 * h + cc].astype(F32)
                for turn in range(4):
                    turned[s, cc, turn] = pltpu.roll(piece, 32 * turn, 1) if turn else piece
        for b in range(4):
            joined = []
            for s in range(2):
                out = turned[s, 0, (0 - b) % 4]
                for cc in range(1, 4):
                    out = jnp.where(lane == cc, turned[s, cc, (cc - b) % 4], out)
                joined.append(out)
            for a in range(2):
                g_ref[r, 2 * (4 * a + b) + h] = jnp.concatenate(
                    [joined[0][8 * a : 8 * a + 8], joined[1][8 * a : 8 * a + 8]], axis=0
                ).astype(BF)
    total = recv0[0].astype(F32)
    for k in range(1, 8):
        total = total + recv0[k].astype(F32)
    g_ref[r, 2 * SLOTS] = total.astype(BF)

    order = [
        zl,
        jnp.where(zl == 0, 1, jnp.where(zl == 1, 0, jnp.where(zl == 2, 1, 2))),
        jnp.where(zl < 2, 2, jnp.where(zl == 2, 3, 1)),
        jnp.where(zl < 2, 3, 0),
    ]

    def block(xx, zz):
        return ((xx + 4) % 4) * 8 + zz * 2 + core

    def to_sibling(ref, n):
        remote(ref, ref, ssib.at[n], rsib.at[n], (sib, c)).start()

    lo = pl.ds(0, HALF)
    hi = pl.ds(HALF, UNITS - HALF)

    def opposite(i, start):
        zz = order[i]
        b = block(x + 2, zz)
        remote(g_ref.at[b, lo], g_ref.at[b, lo], sop.at[zz], rop.at[zz], (sib, c)).wait_recv()
        to_sibling(g_ref.at[b, lo], 12 + zz)
        remote(g_ref.at[b, hi], g_ref.at[b, hi], som.at[zz], rom.at[zz], (sib, c)).wait_recv()
        to_sibling(g_ref.at[b, hi], 16 + zz)

    ups, downs = [], []
    for i in range(4):
        zz = order[i]
        own = g_ref.at[block(x, zz)]
        if i:
            remote(own, own, sz.at[0], rz.at[zz], (sib, c)).wait_recv()
        up = remote(own, own, sz.at[zz], rz.at[zz], (r + 2, c))
        down = remote(own, own, sz.at[4 + zz], rz.at[zz], (r - 2, c))
        goes_up = jnp.logical_and(zz <= zl, zl < 3)
        goes_down = jnp.logical_and(zz >= zl, zl > 0)
        pl.when(goes_up)(up.start)
        pl.when(goes_down)(down.start)
        ups.append((goes_up, up))
        downs.append((goes_down, down))
        remote(own, own, sxp.at[zz], rxp.at[zz], (xp, c)).start()
        remote(own, own, sxm.at[zz], rxm.at[zz], (xm, c)).start()
        to_sibling(own, zz)
        b = block(x - 1, zz)
        remote(g_ref.at[b], g_ref.at[b], sxp.at[zz], rxp.at[zz], (sib, c)).wait_recv()
        remote(g_ref.at[b, lo], g_ref.at[b, lo], sop.at[zz], rop.at[zz], (xp, c)).start()
        to_sibling(g_ref.at[b], 4 + zz)
        b = block(x + 1, zz)
        remote(g_ref.at[b], g_ref.at[b], sxm.at[zz], rxm.at[zz], (sib, c)).wait_recv()
        remote(g_ref.at[b, hi], g_ref.at[b, hi], som.at[zz], rom.at[zz], (xm, c)).start()
        to_sibling(g_ref.at[b], 8 + zz)
        if i:
            opposite(i - 1, False)
    opposite(3, False)

    theirs = 1 - core
    for n in range(20):
        if n < 12:
            b = ((x + (0, 3, 1)[n // 4]) % 4) * 8 + (n % 4) * 2 + theirs
            ref = g_ref.at[b]
        else:
            b = ((x + 2) % 4) * 8 + (n % 4) * 2 + theirs
            ref = g_ref.at[b, lo if n < 16 else hi]
        remote(ref, ref, ssib.at[n], rsib.at[n], (sib, c)).wait_recv()
        remote(ref, ref, ssib.at[n], rsib.at[n], (sib, c)).wait_send()
    for goes, copy in ups + downs:
        pl.when(goes)(copy.wait_send)
    for zz in range(4):
        ref = g_ref.at[0]
        remote(ref, ref, sxp.at[zz], rxp.at[zz], (sib, c)).wait_send()
        remote(ref, ref, sxm.at[zz], rxm.at[zz], (sib, c)).wait_send()
        remote(g_ref.at[0, lo], g_ref.at[0, lo], sop.at[zz], rop.at[zz], (sib, c)).wait_send()
        remote(g_ref.at[0, hi], g_ref.at[0, hi], som.at[zz], rom.at[zz], (sib, c)).wait_send()
    for copy in first:
        copy.wait_send()
    for k, copy in enumerate(lead_copies):
        if k == 0:
            pl.when(half != core)(copy.wait_send)
        else:
            copy.wait_send()
    for load in loads[2:]:
        load.wait()


def apply_kernel(
    starts, flags, q, z, s, t, g, q_out, z_out, s_out, t_out, q_new, z_new, band, q_sem, z_sem, b_sem
):
    r = lax.axis_index("row")
    c = lax.axis_index("col")
    word = slot_words(starts, c)
    count = jnp.int32(0)
    windows = jnp.int32(0)
    for k in range(K):
        mine = (starts[k] >> 13) == c
        count = count + jnp.where(mine, 1, 0)
        bit = jnp.left_shift(jnp.int32(1), (starts[k] >> 8) & (TILES - 1))
        windows = jnp.where(jnp.logical_and(mine, flags[k] == 1), windows | bit, windows)

    def q_copy(src, tile):
        return pltpu.make_async_copy(src, q_out.at[:, pl.ds(pl.multiple_of(tile * W, W), W)], q_sem.at[tile])

    def z_copy(src, tile):
        return pltpu.make_async_copy(src, z_out.at[:, pl.ds(pl.multiple_of(tile * W, W), W)], z_sem.at[tile])

    for tile in range(TILES):

        @pl.when(((windows >> tile) & 1) == 0)
        def _():
            q_copy(q.at[:, pl.ds(tile * W, W)], tile).start()
            z_copy(z.at[:, pl.ds(tile * W, W)], tile).start()

    def factor(side, slot):
        parts = [g[:, side, 2 * slot + h].reshape(W, W // 2) for h in range(2)]
        return jnp.concatenate(parts, axis=1)

    band_slot = jnp.int32(0)
    for j in range(SLOTS):
        k = (word >> (4 * j)) & 15
        tile = (starts[k] >> 8) & (TILES - 1)
        live = jnp.logical_and(j < count, flags[k] == 1)
        band_slot = jnp.where(jnp.logical_and(j < count, tile == r), j, band_slot)

        @pl.when(live)
        def _():
            where = pl.ds(pl.multiple_of(tile * W, W), W)
            q_new[j] = jnp.dot(q[:, where], factor(0, j), preferred_element_type=F32).astype(BF)
            q_copy(q_new.at[j], tile).start()
            z_new[j] = jnp.dot(z[:, where], factor(1, j), preferred_element_type=F32).astype(BF)
            z_copy(z_new.at[j], tile).start()

    band_live = ((windows >> r) & 1) == 1
    right = factor(1, band_slot)
    lead = jnp.concatenate([g[:, h, 2 * SLOTS].reshape(W, W // 2) for h in range(2)], axis=1)
    outs = []
    for i, (ref, out) in enumerate(((s, s_out), (t, t_out))):
        fresh = jnp.dot(ref[...], right, preferred_element_type=F32).astype(BF)
        mid = jnp.where(band_live, fresh, ref[...])
        band[i] = lax.dot_general(
            lead, mid, (((0,), (0,)), ((), ())), preferred_element_type=F32
        ).astype(BF)
        copy = pltpu.make_async_copy(band.at[i], out, b_sem.at[i])
        copy.start()
        outs.append(copy)
    for copy in outs:
        copy.wait()
    for tile in range(TILES):
        q_copy(q.at[:, pl.ds(tile * W, W)], tile).wait()
        z_copy(z.at[:, pl.ds(tile * W, W)], tile).wait()


def local(s_band, t_band, q_rows, z_rows, factors, starts, flags):
    anywhere = pl.BlockSpec(memory_space=pl.ANY)
    vmem = pl.BlockSpec(memory_space=pltpu.VMEM)
    smem = pl.BlockSpec(memory_space=pltpu.SMEM)
    dma = pltpu.SemaphoreType.DMA
    gathered, qv, zv, sv, tv = pl.pallas_call(
        gather_kernel,
        out_shape=(
            pltpu.VMEM((ROWS, UNITS, 16, 128), BF),
            pltpu.VMEM(q_rows.shape, BF),
            pltpu.VMEM(z_rows.shape, BF),
            pltpu.VMEM(s_band.shape, BF),
            pltpu.VMEM(t_band.shape, BF),
        ),
        in_specs=[anywhere] * 6,
        out_specs=[vmem] * 5,
        scratch_shapes=[
            pltpu.SMEM((K,), jnp.int32),
            pltpu.VMEM((K, 2, 8, 32), BF),
            pltpu.VMEM((K, 16, 128), F32),
            pltpu.VMEM((16, 16, 128), BF),
            pltpu.VMEM((16, 16, 128), BF),
            pltpu.VMEM((16, 128), BF),
            pltpu.VMEM((8, 16, 128), BF),
            dma((6,)),
            dma((16,)), dma((16,)), dma((8,)), dma((8,)),
            dma((8,)), dma((4,)),
            dma((4,)), dma((4,)), dma((4,)), dma((4,)),
            dma((4,)), dma((4,)), dma((4,)), dma((4,)),
            dma((20,)), dma((20,)),
        ],
        compiler_params=pltpu.CompilerParams(
            collective_id=0, has_side_effects=True, vmem_limit_bytes=32 << 20
        ),
    )(starts, factors, q_rows, z_rows, s_band, t_band)
    gathered = gathered.reshape(16, 2, UNITS, 16, 128)
    pin = lambda a: pltpu.with_memory_space_constraint(a, pltpu.VMEM)
    return tuple(
        pl.pallas_call(
            apply_kernel,
            out_shape=(
                jax.ShapeDtypeStruct(q_rows.shape, BF),
                jax.ShapeDtypeStruct(z_rows.shape, BF),
                jax.ShapeDtypeStruct(s_band.shape, BF),
                jax.ShapeDtypeStruct(t_band.shape, BF),
            ),
            in_specs=[smem, smem] + [vmem] * 5,
            out_specs=[anywhere] * 4,
            scratch_shapes=[
                pltpu.VMEM((SLOTS, 128, W), BF),
                pltpu.VMEM((SLOTS, 128, W), BF),
                pltpu.VMEM((2, W, W), BF),
                dma((TILES,)),
                dma((TILES,)),
                dma((2,)),
            ],
            compiler_params=pltpu.CompilerParams(vmem_limit_bytes=32 << 20),
        )(starts, flags, *(pin(a) for a in (qv, zv, sv, tv, gathered)))
    )


def solution(mesh):
    in_specs = (
        P(None, ("col", "row")),
        P(None, ("col", "row")),
        P("row", "col"),
        P("row", "col"),
        P(None, None, "row", "col"),
        P(),
        P(),
    )
    out_specs = (P("row", "col"), P("row", "col"), P(None, ("col", "row")), P(None, ("col", "row")))
    return jax.shard_map(local, mesh=mesh, in_specs=in_specs, out_specs=out_specs, check_vma=False)
```

```python
import jax
import jax.numpy as jnp
from jax import lax
from jax.experimental import pallas as pl
from jax.experimental.pallas import tpu as pltpu
from jax.sharding import PartitionSpec as P

W = 256
K = 16
SLOTS = 8
UNITS = 2 * SLOTS + 1
ROWS = 32
COLS = 8
TILES = 32
SPLIT = 12
BF = jnp.bfloat16
F32 = jnp.float32


def slot_words(starts_ref, column):
    word = jnp.int32(0)
    for k in reversed(range(K)):
        mine = (starts_ref[k] >> 13) == column
        word = jnp.where(mine, (word << 4) | k, word)
    return word


def remote(src, dst, send_sem, recv_sem, device):
    return pltpu.make_async_remote_copy(
        src_ref=src,
        dst_ref=dst,
        send_sem=send_sem,
        recv_sem=recv_sem,
        device_id=device,
        device_id_type=pl.DeviceIdType.MESH,
    )


def gather_kernel(
    starts_hbm, factors_hbm, q_hbm, z_hbm, s_hbm, t_hbm,
    g_ref, qv, zv, sv, tv,
    starts_ref, fac, wide, send1, recv1, send0, recv0,
    load_sem, ss1, rs1, ss0, rs0, sza, rza, sxa, rxa, sxb, rxb, szb, rzb, ssib, rsib,
):
    r = lax.axis_index("row")
    c = lax.axis_index("col")
    core = r % 2
    x = r // 8
    zl = (r // 2) % 4
    me = core * 8 + c
    sib = r + 1 - 2 * core
    base = r - core

    barrier = pltpu.get_barrier_semaphore()

    def greet(device):
        pl.semaphore_signal(barrier, inc=1, device_id=device, device_id_type=pl.DeviceIdType.MESH)

    loads = [
        pltpu.make_async_copy(a, b, load_sem.at[i])
        for i, (a, b) in enumerate(
            [(factors_hbm, fac), (starts_hbm, starts_ref), (q_hbm, qv), (z_hbm, zv), (s_hbm, sv), (t_hbm, tv)]
        )
    ]
    loads[0].start()
    loads[1].start()
    for k in range(1, 16):
        other = (me + k) % 16
        greet((base + other // 8, other % 8))
    for k in range(1, 4):
        greet(((r + 8 * k) % ROWS, c))
        greet((x * 8 + (zl + k) % 4 * 2 + core, c))

    wide[...] = jnp.zeros_like(wide)
    loads[0].wait()
    loads[1].wait()
    for load in loads[2:]:
        load.start()
    for k in range(K):
        for m in range(2):
            wide[k, 8 * m : 8 * m + 8, 0:32] = fac[k, m].astype(F32)
    for dest in range(COLS):
        word = slot_words(starts_ref, dest)
        rows = []
        for a in range(2):
            total = None
            for b in range(4):
                k = (word >> (4 * (4 * a + b))) & 15
                piece = wide[k]
                if b:
                    piece = pltpu.roll(piece, 32 * b, 1)
                total = piece if total is None else total + piece
            rows.append(total)
        for m in range(2):
            send1[m * 8 + dest] = jnp.concatenate(
                [rows[0][8 * m : 8 * m + 8], rows[1][8 * m : 8 * m + 8]], axis=0
            ).astype(BF)
    lead = wide[0, 0:8]
    placed = lead
    for b in range(1, 4):
        placed = jnp.where(c % 4 == b, pltpu.roll(lead, 32 * b, 1), placed)
    nothing = jnp.zeros_like(placed)
    send0[...] = jnp.concatenate(
        [jnp.where(core == 0, placed, nothing), jnp.where(core == 1, placed, nothing)], axis=0
    ).astype(BF)

    pl.semaphore_wait(barrier, 21)

    first = []
    for k in range(1, 16):
        other = (me + k) % 16
        copy = remote(send1.at[other], recv1.at[me], ss1.at[k], rs1.at[me], (base + other // 8, other % 8))
        copy.start()
        first.append(copy)
    half = c // 4
    mine0 = core * 4 + c % 4
    lead_copies = []
    for k in range(COLS):
        dest = (c + k) % COLS
        copy = remote(send0, recv0.at[mine0], ss0.at[k], rs0.at[mine0], (base + half, dest))
        if k == 0:
            pl.when(half != core)(copy.start)
        else:
            copy.start()
        lead_copies.append(copy)
    recv1[me] = send1[me]

    @pl.when(half == core)
    def _():
        recv0[mine0] = send0[...]

    for k in range(1, 16):
        other = (me + k) % 16
        remote(recv1.at[other], recv1.at[other], ss1.at[k], rs1.at[other], (sib, c)).wait_recv()
    for k in range(8):
        wait = remote(recv0.at[k], recv0.at[k], ss0.at[0], rs0.at[k], (sib, c)).wait_recv
        pl.when(jnp.logical_or(half != core, k != mine0))(wait)

    lane = lax.broadcasted_iota(jnp.int32, (16, 128), 1) // 32
    for h in range(2):
        turned = {}
        for s in range(2):
            for cc in range(4):
                piece = recv1[s * 8 + 4 * h + cc].astype(F32)
                for turn in range(4):
                    turned[s, cc, turn] = pltpu.roll(piece, 32 * turn, 1) if turn else piece
        for b in range(4):
            joined = []
            for s in range(2):
                out = turned[s, 0, (0 - b) % 4]
                for cc in range(1, 4):
                    out = jnp.where(lane == cc, turned[s, cc, (cc - b) % 4], out)
                joined.append(out)
            for a in range(2):
                g_ref[r, 2 * (4 * a + b) + h] = jnp.concatenate(
                    [joined[0][8 * a : 8 * a + 8], joined[1][8 * a : 8 * a + 8]], axis=0
                ).astype(BF)
    total = recv0[0].astype(F32)
    for k in range(1, 8):
        total = total + recv0[k].astype(F32)
    g_ref[r, 2 * SLOTS] = total.astype(BF)

    order = [
        zl,
        jnp.where(zl == 0, 1, jnp.where(zl == 1, 0, jnp.where(zl == 2, 1, 2))),
        jnp.where(zl < 2, 2, jnp.where(zl == 2, 3, 1)),
        jnp.where(zl < 2, 3, 0),
    ]
    lo = pl.ds(0, SPLIT)
    hi = pl.ds(SPLIT, UNITS - SPLIT)
    ends = []

    def send(ref, send_sem, recv_sem, device):
        copy = remote(ref, ref, send_sem, recv_sem, device)
        copy.start()
        ends.append(copy)

    def got(ref, recv_sem):
        remote(ref, ref, load_sem.at[0], recv_sem, (sib, c)).wait_recv()

    def at(xx, zz, which):
        return g_ref.at[xx * 8 + zz * 2 + core, which]

    xs = [(x + k) % 4 for k in range(4)]
    zs = [(zl + k) % 4 for k in range(4)]

    def along_x(zz, i, which, send_sems, recv_sem):
        for k in (1, 3, 2):
            send(at(x, zz, which), send_sems.at[4 * i + k], recv_sem, (xs[k] * 8 + r % 8, c))

    def along_z(xx, i, which, send_sems, recv_sem):
        for k in (1, 3, 2):
            send(at(xx, zl, which), send_sems.at[4 * i + k], recv_sem, (x * 8 + zs[k] * 2 + core, c))

    def across(xx, zz, which, n):
        spot = 16 * n + xx * 4 + zz
        send(at(xx, zz, which), ssib.at[spot], rsib.at[spot], (sib, c))

    along_z(x, 0, lo, sza, rza.at[zl])
    along_x(zl, 0, hi, sxb, rxb.at[x])
    along_x(zl, 0, lo, sxa, rxa.at[x * 4 + zl])
    along_z(x, 0, hi, szb, rzb.at[x * 4 + zl])
    across(x, zl, lo, 0)
    across(x, zl, hi, 1)
    for i in (1, 2, 3):
        xx = xs[(0, 1, 3, 2)[i]]
        got(at(xx, zl, hi), rxb.at[xx])
        along_z(xx, i, hi, szb, rzb.at[xx * 4 + zl])
        zz = order[i]
        got(at(x, zz, lo), rza.at[zz])
        along_x(zz, i, lo, sxa, rxa.at[x * 4 + zz])
        across(xx, zl, hi, 1)
        across(x, zz, lo, 0)
    for i in range(4):
        for k in (1, 3, 2):
            zz = order[i]
            got(at(xs[k], zz, lo), rxa.at[xs[k] * 4 + zz])
            across(xs[k], zz, lo, 0)
            xx = xs[(0, 1, 3, 2)[i]]
            zz = order[(0, 1, 2, 3)[(0, 1, 3, 2)[k]]]
            got(at(xx, zz, hi), rzb.at[xx * 4 + zz])
            across(xx, zz, hi, 1)

    for spot in range(16):
        b = 2 * spot + 1 - core
        got(g_ref.at[b, lo], rsib.at[spot])
        got(g_ref.at[b, hi], rsib.at[16 + spot])
    for copy in ends:
        copy.wait_send()
    for copy in first:
        copy.wait_send()
    for k, copy in enumerate(lead_copies):
        if k == 0:
            pl.when(half != core)(copy.wait_send)
        else:
            copy.wait_send()
    for load in loads[2:]:
        load.wait()


def apply_kernel(
    starts, flags, q, z, s, t, g, q_out, z_out, s_out, t_out, q_new, z_new, band, q_sem, z_sem, b_sem
):
    r = lax.axis_index("row")
    c = lax.axis_index("col")
    word = slot_words(starts, c)
    count = jnp.int32(0)
    windows = jnp.int32(0)
    for k in range(K):
        mine = (starts[k] >> 13) == c
        count = count + jnp.where(mine, 1, 0)
        bit = jnp.left_shift(jnp.int32(1), (starts[k] >> 8) & (TILES - 1))
        windows = jnp.where(jnp.logical_and(mine, flags[k] == 1), windows | bit, windows)

    def q_copy(src, tile):
        return pltpu.make_async_copy(src, q_out.at[:, pl.ds(pl.multiple_of(tile * W, W), W)], q_sem.at[tile])

    def z_copy(src, tile):
        return pltpu.make_async_copy(src, z_out.at[:, pl.ds(pl.multiple_of(tile * W, W), W)], z_sem.at[tile])

    for tile in range(TILES):

        @pl.when(((windows >> tile) & 1) == 0)
        def _():
            q_copy(q.at[:, pl.ds(tile * W, W)], tile).start()
            z_copy(z.at[:, pl.ds(tile * W, W)], tile).start()

    def factor(side, slot):
        parts = [g[:, side, 2 * slot + h].reshape(W, W // 2) for h in range(2)]
        return jnp.concatenate(parts, axis=1)

    band_slot = jnp.int32(0)
    for j in range(SLOTS):
        k = (word >> (4 * j)) & 15
        tile = (starts[k] >> 8) & (TILES - 1)
        live = jnp.logical_and(j < count, flags[k] == 1)
        band_slot = jnp.where(jnp.logical_and(j < count, tile == r), j, band_slot)

        @pl.when(live)
        def _():
            where = pl.ds(pl.multiple_of(tile * W, W), W)
            q_new[j] = jnp.dot(q[:, where], factor(0, j), preferred_element_type=F32).astype(BF)
            q_copy(q_new.at[j], tile).start()
            z_new[j] = jnp.dot(z[:, where], factor(1, j), preferred_element_type=F32).astype(BF)
            z_copy(z_new.at[j], tile).start()

    band_live = ((windows >> r) & 1) == 1
    right = factor(1, band_slot)
    lead = jnp.concatenate([g[:, h, 2 * SLOTS].reshape(W, W // 2) for h in range(2)], axis=1)
    outs = []
    for i, (ref, out) in enumerate(((s, s_out), (t, t_out))):
        fresh = jnp.dot(ref[...], right, preferred_element_type=F32).astype(BF)
        mid = jnp.where(band_live, fresh, ref[...])
        band[i] = lax.dot_general(
            lead, mid, (((0,), (0,)), ((), ())), preferred_element_type=F32
        ).astype(BF)
        copy = pltpu.make_async_copy(band.at[i], out, b_sem.at[i])
        copy.start()
        outs.append(copy)
    for copy in outs:
        copy.wait()
    for tile in range(TILES):
        q_copy(q.at[:, pl.ds(tile * W, W)], tile).wait()
        z_copy(z.at[:, pl.ds(tile * W, W)], tile).wait()


def local(s_band, t_band, q_rows, z_rows, factors, starts, flags):
    anywhere = pl.BlockSpec(memory_space=pl.ANY)
    hbm = pl.BlockSpec(memory_space=pltpu.HBM)
    vmem = pl.BlockSpec(memory_space=pltpu.VMEM)
    smem = pl.BlockSpec(memory_space=pltpu.SMEM)
    dma = pltpu.SemaphoreType.DMA
    gathered, qv, zv, sv, tv = pl.pallas_call(
        gather_kernel,
        out_shape=(
            pltpu.VMEM((ROWS, UNITS, 16, 128), BF),
            pltpu.VMEM(q_rows.shape, BF),
            pltpu.VMEM(z_rows.shape, BF),
            pltpu.VMEM(s_band.shape, BF),
            pltpu.VMEM(t_band.shape, BF),
        ),
        in_specs=[hbm] * 6,
        out_specs=[vmem] * 5,
        scratch_shapes=[
            pltpu.SMEM((K,), jnp.int32),
            pltpu.VMEM((K, 2, 8, 32), BF),
            pltpu.VMEM((K, 16, 128), F32),
            pltpu.VMEM((16, 16, 128), BF),
            pltpu.VMEM((16, 16, 128), BF),
            pltpu.VMEM((16, 128), BF),
            pltpu.VMEM((8, 16, 128), BF),
            dma((6,)),
            dma((16,)), dma((16,)), dma((8,)), dma((8,)),
            dma((4,)), dma((4,)), dma((16,)), dma((16,)),
            dma((4,)), dma((4,)), dma((16,)), dma((16,)),
            dma((32,)), dma((32,)),
        ],
        compiler_params=pltpu.CompilerParams(
            collective_id=0, has_side_effects=True, vmem_limit_bytes=32 << 20
        ),
    )(*(pltpu.with_memory_space_constraint(a, pltpu.HBM) for a in (starts, factors, q_rows, z_rows, s_band, t_band)))
    gathered = gathered.reshape(16, 2, UNITS, 16, 128)
    pin = lambda a: pltpu.with_memory_space_constraint(a, pltpu.VMEM)
    return tuple(
        pl.pallas_call(
            apply_kernel,
            out_shape=(
                jax.ShapeDtypeStruct(q_rows.shape, BF),
                jax.ShapeDtypeStruct(z_rows.shape, BF),
                jax.ShapeDtypeStruct(s_band.shape, BF),
                jax.ShapeDtypeStruct(t_band.shape, BF),
            ),
            in_specs=[smem, smem] + [vmem] * 5,
            out_specs=[anywhere] * 4,
            scratch_shapes=[
                pltpu.VMEM((SLOTS, 128, W), BF),
                pltpu.VMEM((SLOTS, 128, W), BF),
                pltpu.VMEM((2, W, W), BF),
                dma((TILES,)),
                dma((TILES,)),
                dma((2,)),
            ],
            compiler_params=pltpu.CompilerParams(vmem_limit_bytes=32 << 20),
        )(starts, flags, *(pin(a) for a in (qv, zv, sv, tv, gathered)))
    )


def solution(mesh):
    in_specs = (
        P(None, ("col", "row")),
        P(None, ("col", "row")),
        P("row", "col"),
        P("row", "col"),
        P(None, None, "row", "col"),
        P(),
        P(),
    )
    out_specs = (P("row", "col"), P("row", "col"), P(None, ("col", "row")), P(None, ("col", "row")))
    return jax.shard_map(local, mesh=mesh, in_specs=in_specs, out_specs=out_specs, check_vma=False)
```

```python
import jax
import jax.numpy as jnp
from jax import lax
from jax.experimental import pallas as pl
from jax.experimental.pallas import tpu as pltpu
from jax.sharding import PartitionSpec as P

W = 256
K = 16
SLOTS = 8
UNITS = SLOTS + 1
ROWS = 32
COLS = 8
TILES = 32
SPLIT = 7
BF = jnp.bfloat16
F32 = jnp.float32


def slot_words(starts_ref, column):
    word = jnp.int32(0)
    for k in reversed(range(K)):
        mine = (starts_ref[k] >> 13) == column
        word = jnp.where(mine, (word << 4) | k, word)
    return word


def remote(src, dst, send_sem, recv_sem, device):
    return pltpu.make_async_remote_copy(
        src_ref=src,
        dst_ref=dst,
        send_sem=send_sem,
        recv_sem=recv_sem,
        device_id=device,
        device_id_type=pl.DeviceIdType.MESH,
    )


def gather_kernel(
    starts_hbm, factors_hbm, q_hbm, z_hbm, s_hbm, t_hbm,
    g_ref, qv, zv, sv, tv,
    starts_ref, fac, wide, send1, recv1, send0, recv0,
    load_sem, ss1, rs1, ss0, rs0, sza, rza, sxa, rxa, sxb, rxb, szb, rzb, ssib, rsib,
):
    r = lax.axis_index("row")
    c = lax.axis_index("col")
    core = r % 2
    x = r // 8
    zl = (r // 2) % 4
    far_half = c // 4
    y = c % 4
    me = core * 4 + y
    sib = r + 1 - 2 * core
    near_base = r - core
    far_base = x * 8 + (3 - zl) * 2
    near_col = far_half * 4
    far_col = (1 - far_half) * 4

    barrier = pltpu.get_barrier_semaphore()

    def greet(device):
        pl.semaphore_signal(barrier, inc=1, device_id=device, device_id_type=pl.DeviceIdType.MESH)

    loads = [
        pltpu.make_async_copy(a, b, load_sem.at[i])
        for i, (a, b) in enumerate(
            [(factors_hbm, fac), (starts_hbm, starts_ref), (q_hbm, qv), (z_hbm, zv), (s_hbm, sv), (t_hbm, tv)]
        )
    ]
    loads[0].start()
    loads[1].start()

    @pl.when(far_half == 0)
    def _():
        for k in range(8):
            greet((far_base + k // 4, far_col + k % 4))

    for k in range(1, 8):
        other = (me + k) % 8
        greet((near_base + other // 4, near_col + other % 4))
    for k in range(1, 4):
        greet(((r + 8 * k) % ROWS, c))
        greet((x * 8 + (zl + k) % 4 * 2 + core, c))

    wide[...] = jnp.zeros_like(wide)
    loads[0].wait()
    loads[1].wait()
    for load in loads[2:]:
        load.start()
    for k in range(K):
        for m in range(2):
            wide[k, 8 * m : 8 * m + 8, 0:32] = fac[k, m].astype(F32)
    for wave in (1, 0):
        for dest in range(4):
            word = slot_words(starts_ref, (far_col if wave else near_col) + dest)
            rows = []
            for a in range(2):
                total = None
                for b in range(4):
                    k = (word >> (4 * (4 * a + b))) & 15
                    piece = wide[k]
                    if b:
                        piece = pltpu.roll(piece, 32 * b, 1)
                    total = piece if total is None else total + piece
                rows.append(total)
            for m in range(2):
                send1[wave, m * 4 + dest] = jnp.concatenate(
                    [rows[0][8 * m : 8 * m + 8], rows[1][8 * m : 8 * m + 8]], axis=0
                ).astype(BF)
    lead = wide[0, 0:8]
    placed = lead
    for b in range(1, 4):
        placed = jnp.where(y == b, pltpu.roll(lead, 32 * b, 1), placed)
    nothing = jnp.zeros_like(placed)
    send0[...] = jnp.concatenate(
        [jnp.where(core == 0, placed, nothing), jnp.where(core == 1, placed, nothing)], axis=0
    ).astype(BF)

    def far_piece(k):
        device = (far_base + k // 4, far_col + k % 4)
        return remote(send1.at[1, k], recv1.at[1, me], ss1.at[8 + k], rs1.at[8 + me], device)

    def far_lead(k):
        return remote(send0, recv0.at[me], ss0.at[4 + k], rs0.at[me], (far_base + 1, far_col + k))

    def near_piece(k):
        other = (me + k) % 8
        device = (near_base + other // 4, near_col + other % 4)
        return remote(send1.at[0, other], recv1.at[0, me], ss1.at[k], rs1.at[me], device)

    def near_lead(k):
        return remote(send0, recv0.at[me], ss0.at[k], rs0.at[me], (near_base, near_col + (y + k) % 4))

    def got(ref, recv_sem):
        remote(ref, ref, load_sem.at[0], recv_sem, (sib, c)).wait_recv()

    @pl.when(far_half == 1)
    def _():
        pl.semaphore_wait(barrier, 21)
        for k in range(8):
            far_piece(k).start()
        for k in range(4):
            far_lead(k).start()

    @pl.when(far_half == 0)
    def _():
        pl.semaphore_wait(barrier, 13)

    for k in range(1, 8):
        near_piece(k).start()
    pl.when(core == 1)(near_lead(0).start)
    for k in range(1, 4):
        near_lead(k).start()
    recv1[0, me] = send1[0, me]

    @pl.when(core == 0)
    def _():
        recv0[me] = send0[...]

    lane = lax.broadcasted_iota(jnp.int32, (16, 128), 1) // 32

    def unpack(wave):
        spot = far_base + core if wave else r
        turned = {}
        for s in range(2):
            for cc in range(4):
                piece = recv1[wave, s * 4 + cc].astype(F32)
                for turn in range(4):
                    turned[s, cc, turn] = pltpu.roll(piece, 32 * turn, 1) if turn else piece
        for b in range(4):
            joined = []
            for s in range(2):
                out = turned[s, 0, (0 - b) % 4]
                for cc in range(1, 4):
                    out = jnp.where(lane == cc, turned[s, cc, (cc - b) % 4], out)
                joined.append(out)
            for a in range(2):
                g_ref[wave, spot, 4 * a + b] = jnp.concatenate(
                    [joined[0][8 * a : 8 * a + 8], joined[1][8 * a : 8 * a + 8]], axis=0
                ).astype(BF)

        @pl.when(core == wave)
        def _():
            total = recv0[0].astype(F32)
            for k in range(1, 8):
                total = total + recv0[k].astype(F32)
            g_ref[wave, spot, SLOTS] = total.astype(BF)

        @pl.when(core != wave)
        def _():
            g_ref[wave, spot, SLOTS] = jnp.zeros((16, 128), BF)

    order = [
        zl,
        jnp.where(zl == 0, 1, jnp.where(zl == 1, 0, jnp.where(zl == 2, 1, 2))),
        jnp.where(zl < 2, 2, jnp.where(zl == 2, 3, 1)),
        jnp.where(zl < 2, 3, 0),
    ]
    lo = pl.ds(0, SPLIT)
    hi = pl.ds(SPLIT, UNITS - SPLIT)
    xs = [(x + k) % 4 for k in range(4)]
    zs = [(zl + k) % 4 for k in range(4)]
    nearest = (0, 1, 3, 2)

    def at(wave, xx, zz, which):
        return g_ref.at[wave, xx * 8 + (3 - zz if wave else zz) * 2 + core, which]

    def send(ref, send_sem, recv_sem, device):
        remote(ref, ref, send_sem, recv_sem, device).start()

    def along_x(wave, zz, i, which, send_sems, recv_sem):
        for k in (1, 3, 2):
            send(at(wave, x, zz, which), send_sems.at[wave, 4 * i + k], recv_sem, (xs[k] * 8 + r % 8, c))

    def along_z(wave, xx, i, which, send_sems, recv_sem):
        for k in (1, 3, 2):
            device = (x * 8 + zs[k] * 2 + core, c)
            send(at(wave, xx, zl, which), send_sems.at[wave, 4 * i + k], recv_sem, device)

    def across(wave, xx, zz, which, n):
        spot = 16 * n + xx * 4 + zz
        send(at(wave, xx, zz, which), ssib.at[wave, spot], rsib.at[wave, spot], (sib, c))

    def first_leg(wave):
        along_z(wave, x, 0, lo, sza, rza.at[wave, zl])
        along_x(wave, zl, 0, hi, sxb, rxb.at[wave, x])
        along_x(wave, zl, 0, lo, sxa, rxa.at[wave, x * 4 + zl])
        along_z(wave, x, 0, hi, szb, rzb.at[wave, x * 4 + zl])
        across(wave, x, zl, lo, 0)
        across(wave, x, zl, hi, 1)

    def second_leg(wave):
        for i in (1, 2, 3):
            xx = xs[nearest[i]]
            got(at(wave, xx, zl, hi), rxb.at[wave, xx])
            along_z(wave, xx, i, hi, szb, rzb.at[wave, xx * 4 + zl])
            zz = order[i]
            got(at(wave, x, zz, lo), rza.at[wave, zz])
            along_x(wave, zz, i, lo, sxa, rxa.at[wave, x * 4 + zz])
            across(wave, xx, zl, hi, 1)
            across(wave, x, zz, lo, 0)

    def last_leg(wave):
        for i in range(4):
            for k in (1, 2, 3):
                zz, xx = order[i], xs[nearest[k]]
                got(at(wave, xx, zz, lo), rxa.at[wave, xx * 4 + zz])
                across(wave, xx, zz, lo, 0)
                zz, xx = order[k], xs[nearest[i]]
                got(at(wave, xx, zz, hi), rzb.at[wave, xx * 4 + zz])
                across(wave, xx, zz, hi, 1)

    for k in range(1, 8):
        other = (me + k) % 8
        got(recv1.at[0, other], rs1.at[other])

    @pl.when(core == 0)
    def _():
        for k in range(1, 8):
            other = (me + k) % 8
            got(recv0.at[other], rs0.at[other])

    unpack(0)
    first_leg(0)

    @pl.when(far_half == 1)
    def _():
        second_leg(0)

    for k in range(8):
        got(recv1.at[1, k], rs1.at[8 + k])

        @pl.when(far_half == 0)
        def _():
            far_piece(k).start()
            if k >= 4:
                far_lead(k - 4).start()

    @pl.when(core == 1)
    def _():
        for k in range(8):
            got(recv0.at[k], rs0.at[k])

    unpack(1)
    first_leg(1)

    @pl.when(far_half == 0)
    def _():
        second_leg(0)

    second_leg(1)
    last_leg(0)
    last_leg(1)

    for wave in range(2):
        for spot in range(16):
            zz = spot % 4
            b = (spot // 4) * 8 + (3 - zz if wave else zz) * 2 + 1 - core
            got(g_ref.at[wave, b, lo], rsib.at[wave, spot])
            got(g_ref.at[wave, b, hi], rsib.at[wave, 16 + spot])

    def left(ref, send_sem):
        remote(ref, ref, send_sem, load_sem.at[0], (sib, c)).wait_send()

    for wave in range(2):
        small, large = g_ref.at[wave, 0, hi], g_ref.at[wave, 0, lo]
        for k in (1, 2, 3):
            left(large, sza.at[wave, k])
            left(small, sxb.at[wave, k])
            for i in range(4):
                left(large, sxa.at[wave, 4 * i + k])
                left(small, szb.at[wave, 4 * i + k])
        for spot in range(16):
            left(large, ssib.at[wave, spot])
            left(small, ssib.at[wave, 16 + spot])
    for k in range(8):
        left(send1.at[1, k], ss1.at[8 + k])
        if k:
            left(send1.at[0, k], ss1.at[k])
    for k in range(8):
        if k:
            left(send0, ss0.at[k])
        else:
            pl.when(core == 1)(near_lead(0).wait_send)
    for load in loads[2:]:
        load.wait()


def apply_kernel(
    starts, flags, q, z, s, t, g, q_out, z_out, s_out, t_out, q_new, z_new, band, q_sem, z_sem, b_sem, whole_sem
):
    r = lax.axis_index("row")
    c = lax.axis_index("col")
    word = slot_words(starts, c)
    count = jnp.int32(0)
    windows = jnp.int32(0)
    for k in range(K):
        mine = (starts[k] >> 13) == c
        count = count + jnp.where(mine, 1, 0)
        bit = jnp.left_shift(jnp.int32(1), (starts[k] >> 8) & (TILES - 1))
        windows = jnp.where(jnp.logical_and(mine, flags[k] == 1), windows | bit, windows)

    wholes = [pltpu.make_async_copy(q, q_out, whole_sem.at[0]), pltpu.make_async_copy(z, z_out, whole_sem.at[1])]
    for whole in wholes:
        whole.start()

    def q_copy(j, tile):
        return pltpu.make_async_copy(q_new.at[j], q_out.at[:, pl.ds(pl.multiple_of(tile * W, W), W)], q_sem.at[j])

    def z_copy(j, tile):
        return pltpu.make_async_copy(z_new.at[j], z_out.at[:, pl.ds(pl.multiple_of(tile * W, W), W)], z_sem.at[j])

    far_half = c // 4

    def factor(side, slot):
        parts = [g[h ^ far_half, :, side, slot].reshape(W, W // 2) for h in range(2)]
        return jnp.concatenate(parts, axis=1)

    band_slot = jnp.int32(0)
    slots = []
    for j in range(SLOTS):
        k = (word >> (4 * j)) & 15
        tile = (starts[k] >> 8) & (TILES - 1)
        live = jnp.logical_and(j < count, flags[k] == 1)
        band_slot = jnp.where(jnp.logical_and(j < count, tile == r), j, band_slot)
        slots.append((live, tile))

        @pl.when(live)
        def _():
            where = pl.ds(pl.multiple_of(tile * W, W), W)
            q_new[j] = jnp.dot(q[:, where], factor(0, j), preferred_element_type=F32).astype(BF)
            z_new[j] = jnp.dot(z[:, where], factor(1, j), preferred_element_type=F32).astype(BF)

    band_live = ((windows >> r) & 1) == 1
    right = factor(1, band_slot)
    lead = jnp.concatenate(
        [g[h ^ far_half, :, h ^ far_half, SLOTS].reshape(W, W // 2) for h in range(2)], axis=1
    )
    outs = []
    for i, (ref, out) in enumerate(((s, s_out), (t, t_out))):
        fresh = jnp.dot(ref[...], right, preferred_element_type=F32).astype(BF)
        mid = jnp.where(band_live, fresh, ref[...])
        band[i] = lax.dot_general(
            lead, mid, (((0,), (0,)), ((), ())), preferred_element_type=F32
        ).astype(BF)
        copy = pltpu.make_async_copy(band.at[i], out, b_sem.at[i])
        copy.start()
        outs.append(copy)
    for whole in wholes:
        whole.wait()
    for j, (live, tile) in enumerate(slots):

        @pl.when(live)
        def _():
            q_copy(j, tile).start()
            z_copy(j, tile).start()

    for copy in outs:
        copy.wait()
    for j, (live, tile) in enumerate(slots):

        @pl.when(live)
        def _():
            q_copy(j, tile).wait()
            z_copy(j, tile).wait()


def local(s_band, t_band, q_rows, z_rows, factors, starts, flags):
    anywhere = pl.BlockSpec(memory_space=pl.ANY)
    hbm = pl.BlockSpec(memory_space=pltpu.HBM)
    vmem = pl.BlockSpec(memory_space=pltpu.VMEM)
    smem = pl.BlockSpec(memory_space=pltpu.SMEM)
    dma = pltpu.SemaphoreType.DMA
    gathered, qv, zv, sv, tv = pl.pallas_call(
        gather_kernel,
        out_shape=(
            pltpu.VMEM((2, ROWS, UNITS, 16, 128), BF),
            pltpu.VMEM(q_rows.shape, BF),
            pltpu.VMEM(z_rows.shape, BF),
            pltpu.VMEM(s_band.shape, BF),
            pltpu.VMEM(t_band.shape, BF),
        ),
        in_specs=[hbm] * 6,
        out_specs=[vmem] * 5,
        scratch_shapes=[
            pltpu.SMEM((K,), jnp.int32),
            pltpu.VMEM((K, 2, 8, 32), BF),
            pltpu.VMEM((K, 16, 128), F32),
            pltpu.VMEM((2, 8, 16, 128), BF),
            pltpu.VMEM((2, 8, 16, 128), BF),
            pltpu.VMEM((16, 128), BF),
            pltpu.VMEM((8, 16, 128), BF),
            dma((6,)),
            dma((16,)), dma((16,)), dma((8,)), dma((8,)),
            dma((2, 4)), dma((2, 4)), dma((2, 16)), dma((2, 16)),
            dma((2, 4)), dma((2, 4)), dma((2, 16)), dma((2, 16)),
            dma((2, 32)), dma((2, 32)),
        ],
        compiler_params=pltpu.CompilerParams(
            collective_id=0, has_side_effects=True, vmem_limit_bytes=32 << 20
        ),
    )(*(pltpu.with_memory_space_constraint(a, pltpu.HBM) for a in (starts, factors, q_rows, z_rows, s_band, t_band)))
    gathered = gathered.reshape(2, 16, 2, UNITS, 16, 128)
    pin = lambda a: pltpu.with_memory_space_constraint(a, pltpu.VMEM)
    return tuple(
        pl.pallas_call(
            apply_kernel,
            out_shape=(
                jax.ShapeDtypeStruct(q_rows.shape, BF),
                jax.ShapeDtypeStruct(z_rows.shape, BF),
                jax.ShapeDtypeStruct(s_band.shape, BF),
                jax.ShapeDtypeStruct(t_band.shape, BF),
            ),
            in_specs=[smem, smem] + [vmem] * 5,
            out_specs=[anywhere] * 4,
            scratch_shapes=[
                pltpu.VMEM((SLOTS, 128, W), BF),
                pltpu.VMEM((SLOTS, 128, W), BF),
                pltpu.VMEM((2, W, W), BF),
                dma((SLOTS,)),
                dma((SLOTS,)),
                dma((2,)),
                dma((2,)),
            ],
            compiler_params=pltpu.CompilerParams(vmem_limit_bytes=32 << 20),
        )(starts, flags, *(pin(a) for a in (qv, zv, sv, tv, gathered)))
    )


def solution(mesh):
    in_specs = (
        P(None, ("col", "row")),
        P(None, ("col", "row")),
        P("row", "col"),
        P("row", "col"),
        P(None, None, "row", "col"),
        P(),
        P(),
    )
    out_specs = (P("row", "col"), P("row", "col"), P(None, ("col", "row")), P(None, ("col", "row")))
    return jax.shard_map(local, mesh=mesh, in_specs=in_specs, out_specs=out_specs, check_vma=False)
```

```python
import jax
import jax.numpy as jnp
from jax import lax
from jax.experimental import pallas as pl
from jax.experimental.pallas import tpu as pltpu
from jax.sharding import PartitionSpec as P

W = 256
K = 16
SLOTS = 8
UNITS = SLOTS + 1
ROWS = 32
COLS = 8
TILES = 32
SPLIT = 7
BF = jnp.bfloat16
F32 = jnp.float32


def slot_words(starts_ref, column):
    word = jnp.int32(0)
    for k in reversed(range(K)):
        mine = (starts_ref[k] >> 13) == column
        word = jnp.where(mine, (word << 4) | k, word)
    return word


def remote(src, dst, send_sem, recv_sem, device):
    return pltpu.make_async_remote_copy(
        src_ref=src,
        dst_ref=dst,
        send_sem=send_sem,
        recv_sem=recv_sem,
        device_id=device,
        device_id_type=pl.DeviceIdType.MESH,
    )


def gather_kernel(
    starts_hbm, factors_hbm, q_hbm, z_hbm, s_hbm, t_hbm,
    g_ref, qv, zv, sv, tv,
    starts_ref, fac, wide, send1, recv1, send0, recv0,
    load_sem, sent1, sent0, came1, came0, sent, line_sem, ring_sem, group_sem, sib_sem,
):
    r = lax.axis_index("row")
    c = lax.axis_index("col")
    core = r % 2
    x = r // 8
    zl = (r // 2) % 4
    far_half = c // 4
    y = c % 4
    me = core * 4 + y
    sib = r + 1 - 2 * core
    near_base = r - core
    far_base = x * 8 + (3 - zl) * 2
    near_col = far_half * 4
    far_col = (1 - far_half) * 4

    barrier = pltpu.get_barrier_semaphore()

    def greet(device):
        pl.semaphore_signal(barrier, inc=1, device_id=device, device_id_type=pl.DeviceIdType.MESH)

    loads = [
        pltpu.make_async_copy(a, b, load_sem.at[i])
        for i, (a, b) in enumerate(
            [(factors_hbm, fac), (starts_hbm, starts_ref), (q_hbm, qv), (z_hbm, zv), (s_hbm, sv), (t_hbm, tv)]
        )
    ]
    loads[0].start()
    loads[1].start()

    @pl.when(far_half == 0)
    def _():
        for k in range(8):
            greet((far_base + k // 4, far_col + k % 4))

    for k in range(1, 8):
        other = (me + k) % 8
        greet((near_base + other // 4, near_col + other % 4))
    for k in range(1, 4):
        greet(((r + 8 * k) % ROWS, c))
        greet((x * 8 + (zl + k) % 4 * 2 + core, c))

    wide[...] = jnp.zeros_like(wide)
    loads[0].wait()
    loads[1].wait()
    for load in loads[2:]:
        load.start()
    for k in range(K):
        for m in range(2):
            wide[k, 8 * m : 8 * m + 8, 0:32] = fac[k, m].astype(F32)
    for wave in (1, 0):
        for dest in range(4):
            word = slot_words(starts_ref, (far_col if wave else near_col) + dest)
            rows = []
            for a in range(2):
                total = None
                for b in range(4):
                    k = (word >> (4 * (4 * a + b))) & 15
                    piece = wide[k]
                    if b:
                        piece = pltpu.roll(piece, 32 * b, 1)
                    total = piece if total is None else total + piece
                rows.append(total)
            for m in range(2):
                send1[wave, m * 4 + dest] = jnp.concatenate(
                    [rows[0][8 * m : 8 * m + 8], rows[1][8 * m : 8 * m + 8]], axis=0
                ).astype(BF)
    lead = wide[0, 0:8]
    placed = lead
    for b in range(1, 4):
        placed = jnp.where(y == b, pltpu.roll(lead, 32 * b, 1), placed)
    nothing = jnp.zeros_like(placed)
    send0[...] = jnp.concatenate(
        [jnp.where(core == 0, placed, nothing), jnp.where(core == 1, placed, nothing)], axis=0
    ).astype(BF)

    def far_piece(k):
        device = (far_base + k // 4, far_col + k % 4)
        return remote(send1.at[1, k], recv1.at[1, me], sent1.at[1], came1.at[1], device)

    def far_lead(k):
        return remote(send0, recv0.at[me], sent0.at[1], came0, (far_base + 1, far_col + k))

    def near_piece(k):
        other = (me + k) % 8
        device = (near_base + other // 4, near_col + other % 4)
        return remote(send1.at[0, other], recv1.at[0, me], sent1.at[0], came1.at[0], device)

    def near_lead(k):
        sem = sent0.at[0] if k else sent0.at[2]
        return remote(send0, recv0.at[me], sem, came0, (near_base, near_col + (y + k) % 4))

    def got(ref, recv_sem):
        remote(ref, ref, load_sem.at[0], recv_sem, (sib, c)).wait_recv()

    @pl.when(far_half == 1)
    def _():
        pl.semaphore_wait(barrier, 21)
        for k in range(8):
            far_piece(k).start()
        for k in range(4):
            far_lead(k).start()

    @pl.when(far_half == 0)
    def _():
        pl.semaphore_wait(barrier, 13)

    for k in range(1, 8):
        near_piece(k).start()
    pl.when(core == 1)(near_lead(0).start)
    for k in range(1, 4):
        near_lead(k).start()
    recv1[0, me] = send1[0, me]

    @pl.when(core == 0)
    def _():
        recv0[me] = send0[...]

    lane = lax.broadcasted_iota(jnp.int32, (16, 128), 1) // 32

    def unpack(wave):
        spot = far_base + core if wave else r
        turned = {}
        for s in range(2):
            for cc in range(4):
                piece = recv1[wave, s * 4 + cc].astype(F32)
                for turn in range(4):
                    turned[s, cc, turn] = pltpu.roll(piece, 32 * turn, 1) if turn else piece
        for b in range(4):
            joined = []
            for s in range(2):
                out = turned[s, 0, (0 - b) % 4]
                for cc in range(1, 4):
                    out = jnp.where(lane == cc, turned[s, cc, (cc - b) % 4], out)
                joined.append(out)
            for a in range(2):
                g_ref[wave, spot, 4 * a + b] = jnp.concatenate(
                    [joined[0][8 * a : 8 * a + 8], joined[1][8 * a : 8 * a + 8]], axis=0
                ).astype(BF)

        @pl.when(core == wave)
        def _():
            total = recv0[0].astype(F32)
            for k in range(1, 8):
                total = total + recv0[k].astype(F32)
            g_ref[wave, spot, SLOTS] = total.astype(BF)

        @pl.when(core != wave)
        def _():
            g_ref[wave, spot, SLOTS] = jnp.zeros((16, 128), BF)

    order = [
        zl,
        jnp.where(zl == 0, 1, jnp.where(zl == 1, 0, jnp.where(zl == 2, 1, 2))),
        jnp.where(zl < 2, 2, jnp.where(zl == 2, 3, 1)),
        jnp.where(zl < 2, 3, 0),
    ]
    lo = pl.ds(0, SPLIT)
    hi = pl.ds(SPLIT, UNITS - SPLIT)
    whole = pl.ds(0, UNITS)
    xs = [(x + k) % 4 for k in range(4)]
    zs = [(zl + k) % 4 for k in range(4)]
    nearest = (0, 1, 3, 2)

    def at(wave, xx, zz, which):
        return g_ref.at[wave, xx * 8 + (3 - zz if wave else zz) * 2 + core, which]

    def send(ref, recv_sem, device, wave):
        remote(ref, ref, sent.at[wave], recv_sem, device).start()

    def along_x(wave, zz, which, recv_sem):
        for k in (1, 3, 2):
            send(at(wave, x, zz, which), recv_sem, (xs[k] * 8 + r % 8, c), wave)

    def along_z(wave, xx, which, recv_sem):
        for k in (1, 3, 2):
            send(at(wave, xx, zl, which), recv_sem, (x * 8 + zs[k] * 2 + core, c), wave)

    def across(wave, xx, zz, which):
        send(at(wave, xx, zz, which), sib_sem.at[wave], (sib, c), wave)

    def first_leg(wave):
        along_z(wave, x, lo, line_sem.at[wave, zl])
        along_x(wave, zl, hi, ring_sem.at[wave, x])
        along_x(wave, zl, lo, group_sem.at[wave, 0])
        along_z(wave, x, hi, group_sem.at[wave, 0])
        across(wave, x, zl, whole)

    def second_leg(wave):
        for i in (1, 2, 3):
            xx = xs[nearest[i]]
            got(at(wave, xx, zl, hi), ring_sem.at[wave, xx])
            along_z(wave, xx, hi, group_sem.at[wave, i])
            zz = order[i]
            got(at(wave, x, zz, lo), line_sem.at[wave, zz])
            along_x(wave, zz, lo, group_sem.at[wave, i])
            across(wave, xx, zl, hi)
            across(wave, x, zz, lo)

    def last_leg(wave):
        for i in range(4):
            got(g_ref.at[wave, pl.ds(0, 3)], group_sem.at[wave, i])
            for k in (1, 2, 3):
                across(wave, xs[nearest[k]], order[i], lo)
                across(wave, xs[nearest[i]], order[k], hi)

    got(recv1.at[0, pl.ds(0, 7)], came1.at[0])

    @pl.when(core == 0)
    def _():
        got(recv0.at[pl.ds(0, 7)], came0)

    unpack(0)
    first_leg(0)

    @pl.when(far_half == 1)
    def _():
        second_leg(0)

    got(recv1.at[1], came1.at[1])

    @pl.when(far_half == 0)
    def _():
        for k in range(8):
            far_piece(k).start()
        for k in range(4):
            far_lead(k).start()

    @pl.when(core == 1)
    def _():
        got(recv0, came0)

    unpack(1)
    first_leg(1)

    @pl.when(far_half == 0)
    def _():
        second_leg(0)

    second_leg(1)
    last_leg(0)
    last_leg(1)

    for wave in range(2):
        got(g_ref.at[wave, pl.ds(0, 16)], sib_sem.at[wave])

    def left(ref, send_sem):
        remote(ref, ref, send_sem, load_sem.at[0], (sib, c)).wait_send()

    for wave in range(2):
        left(g_ref.at[wave, pl.ds(0, 31)], sent.at[wave])
    left(send1.at[0, pl.ds(0, 7)], sent1.at[0])
    left(send1.at[1], sent1.at[1])
    left(recv0.at[pl.ds(0, 3)], sent0.at[0])
    left(recv0.at[pl.ds(0, 4)], sent0.at[1])
    pl.when(core == 1)(near_lead(0).wait_send)
    for load in loads[2:]:
        load.wait()


def apply_kernel(
    starts, flags, q, z, s, t, g, q_out, z_out, s_out, t_out, q_new, z_new, band, q_sem, z_sem, b_sem, whole_sem
):
    r = lax.axis_index("row")
    c = lax.axis_index("col")
    word = slot_words(starts, c)
    count = jnp.int32(0)
    windows = jnp.int32(0)
    for k in range(K):
        mine = (starts[k] >> 13) == c
        count = count + jnp.where(mine, 1, 0)
        bit = jnp.left_shift(jnp.int32(1), (starts[k] >> 8) & (TILES - 1))
        windows = jnp.where(jnp.logical_and(mine, flags[k] == 1), windows | bit, windows)

    wholes = [pltpu.make_async_copy(q, q_out, whole_sem.at[0]), pltpu.make_async_copy(z, z_out, whole_sem.at[1])]
    for whole in wholes:
        whole.start()

    def q_copy(j, tile):
        return pltpu.make_async_copy(q_new.at[j], q_out.at[:, pl.ds(pl.multiple_of(tile * W, W), W)], q_sem.at[j])

    def z_copy(j, tile):
        return pltpu.make_async_copy(z_new.at[j], z_out.at[:, pl.ds(pl.multiple_of(tile * W, W), W)], z_sem.at[j])

    far_half = c // 4

    def factor(side, slot):
        parts = [g[h ^ far_half, :, side, slot].reshape(W, W // 2) for h in range(2)]
        return jnp.concatenate(parts, axis=1)

    band_slot = jnp.int32(0)
    slots = []
    for j in range(SLOTS):
        k = (word >> (4 * j)) & 15
        tile = (starts[k] >> 8) & (TILES - 1)
        live = jnp.logical_and(j < count, flags[k] == 1)
        band_slot = jnp.where(jnp.logical_and(j < count, tile == r), j, band_slot)
        slots.append((live, tile))

        @pl.when(live)
        def _():
            where = pl.ds(pl.multiple_of(tile * W, W), W)
            q_new[j] = jnp.dot(q[:, where], factor(0, j), preferred_element_type=F32).astype(BF)
            z_new[j] = jnp.dot(z[:, where], factor(1, j), preferred_element_type=F32).astype(BF)

    band_live = ((windows >> r) & 1) == 1
    right = factor(1, band_slot)
    lead = jnp.concatenate(
        [g[h ^ far_half, :, h ^ far_half, SLOTS].reshape(W, W // 2) for h in range(2)], axis=1
    )
    outs = []
    for i, (ref, out) in enumerate(((s, s_out), (t, t_out))):
        fresh = jnp.dot(ref[...], right, preferred_element_type=F32).astype(BF)
        mid = jnp.where(band_live, fresh, ref[...])
        band[i] = lax.dot_general(
            lead, mid, (((0,), (0,)), ((), ())), preferred_element_type=F32
        ).astype(BF)
        copy = pltpu.make_async_copy(band.at[i], out, b_sem.at[i])
        copy.start()
        outs.append(copy)
    for whole in wholes:
        whole.wait()
    for j, (live, tile) in enumerate(slots):

        @pl.when(live)
        def _():
            q_copy(j, tile).start()
            z_copy(j, tile).start()

    for copy in outs:
        copy.wait()
    for j, (live, tile) in enumerate(slots):

        @pl.when(live)
        def _():
            q_copy(j, tile).wait()
            z_copy(j, tile).wait()


def local(s_band, t_band, q_rows, z_rows, factors, starts, flags):
    anywhere = pl.BlockSpec(memory_space=pl.ANY)
    hbm = pl.BlockSpec(memory_space=pltpu.HBM)
    vmem = pl.BlockSpec(memory_space=pltpu.VMEM)
    smem = pl.BlockSpec(memory_space=pltpu.SMEM)
    dma = pltpu.SemaphoreType.DMA
    gathered, qv, zv, sv, tv = pl.pallas_call(
        gather_kernel,
        out_shape=(
            pltpu.VMEM((2, ROWS, UNITS, 16, 128), BF),
            pltpu.VMEM(q_rows.shape, BF),
            pltpu.VMEM(z_rows.shape, BF),
            pltpu.VMEM(s_band.shape, BF),
            pltpu.VMEM(t_band.shape, BF),
        ),
        in_specs=[hbm] * 6,
        out_specs=[vmem] * 5,
        scratch_shapes=[
            pltpu.SMEM((K,), jnp.int32),
            pltpu.VMEM((K, 2, 8, 32), BF),
            pltpu.VMEM((K, 16, 128), F32),
            pltpu.VMEM((2, 8, 16, 128), BF),
            pltpu.VMEM((2, 8, 16, 128), BF),
            pltpu.VMEM((16, 128), BF),
            pltpu.VMEM((8, 16, 128), BF),
            dma((6,)),
            dma((2,)), dma((3,)), dma((2,)), dma(()),
            dma((2,)), dma((2, 4)), dma((2, 4)), dma((2, 4)), dma((2,)),
        ],
        compiler_params=pltpu.CompilerParams(
            collective_id=0, has_side_effects=True, vmem_limit_bytes=32 << 20
        ),
    )(*(pltpu.with_memory_space_constraint(a, pltpu.HBM) for a in (starts, factors, q_rows, z_rows, s_band, t_band)))
    gathered = gathered.reshape(2, 16, 2, UNITS, 16, 128)
    pin = lambda a: pltpu.with_memory_space_constraint(a, pltpu.VMEM)
    return tuple(
        pl.pallas_call(
            apply_kernel,
            out_shape=(
                jax.ShapeDtypeStruct(q_rows.shape, BF),
                jax.ShapeDtypeStruct(z_rows.shape, BF),
                jax.ShapeDtypeStruct(s_band.shape, BF),
                jax.ShapeDtypeStruct(t_band.shape, BF),
            ),
            in_specs=[smem, smem] + [vmem] * 5,
            out_specs=[anywhere] * 4,
            scratch_shapes=[
                pltpu.VMEM((SLOTS, 128, W), BF),
                pltpu.VMEM((SLOTS, 128, W), BF),
                pltpu.VMEM((2, W, W), BF),
                dma((SLOTS,)),
                dma((SLOTS,)),
                dma((2,)),
                dma((2,)),
            ],
            compiler_params=pltpu.CompilerParams(vmem_limit_bytes=32 << 20),
        )(starts, flags, *(pin(a) for a in (qv, zv, sv, tv, gathered)))
    )


def solution(mesh):
    in_specs = (
        P(None, ("col", "row")),
        P(None, ("col", "row")),
        P("row", "col"),
        P("row", "col"),
        P(None, None, "row", "col"),
        P(),
        P(),
    )
    out_specs = (P("row", "col"), P("row", "col"), P(None, ("col", "row")), P(None, ("col", "row")))
    return jax.shard_map(local, mesh=mesh, in_specs=in_specs, out_specs=out_specs, check_vma=False)
```

```python
import jax
import jax.numpy as jnp
from jax import lax
from jax.experimental import pallas as pl
from jax.experimental.pallas import tpu as pltpu
from jax.sharding import PartitionSpec as P

W = 256
K = 16
SLOTS = 8
UNITS = SLOTS + 1
ROWS = 32
COLS = 8
TILES = 32
SPLITS = (7, 6)
EARLY = 0
PARTS = 4
BF = jnp.bfloat16
F32 = jnp.float32


def slot_words(starts_ref, column):
    word = jnp.int32(0)
    for k in reversed(range(K)):
        mine = (starts_ref[k] >> 13) == column
        word = jnp.where(mine, (word << 4) | k, word)
    return word


def remote(src, dst, send_sem, recv_sem, device):
    return pltpu.make_async_remote_copy(
        src_ref=src,
        dst_ref=dst,
        send_sem=send_sem,
        recv_sem=recv_sem,
        device_id=device,
        device_id_type=pl.DeviceIdType.MESH,
    )


def gather_kernel(
    starts_hbm, factors_hbm, q_hbm, z_hbm, s_hbm, t_hbm, q_copied, z_copied,
    g_ref, qv, zv, sv, tv,
    starts_ref, fac, wide, send1, recv1, send0, recv0,
    load_sem, sent1, sent0, came1, came0, sent, line_sem, ring_sem, group_sem, sib_sem, far_sem,
):
    r = lax.axis_index("row")
    c = lax.axis_index("col")
    core = r % 2
    x = r // 8
    zl = (r // 2) % 4
    far_half = c // 4
    y = c % 4
    me = core * 4 + y
    sib = r + 1 - 2 * core
    near_base = r - core
    far_base = x * 8 + (3 - zl) * 2
    near_col = far_half * 4
    far_col = (1 - far_half) * 4

    barrier = pltpu.get_barrier_semaphore()

    def greet(device):
        pl.semaphore_signal(barrier, inc=1, device_id=device, device_id_type=pl.DeviceIdType.MESH)

    loads = [
        pltpu.make_async_copy(a, b, load_sem.at[i])
        for i, (a, b) in enumerate(
            [(factors_hbm, fac), (starts_hbm, starts_ref), (q_hbm, qv), (z_hbm, zv), (s_hbm, sv), (t_hbm, tv)]
        )
    ]
    loads[0].start()
    loads[1].start()

    @pl.when(far_half == 0)
    def _():
        for k in range(8):
            greet((far_base + k // 4, far_col + k % 4))

    for k in (3, 1, 2):
        greet((x * 8 + (zl + k) % 4 * 2 + core, c))
    for k in (4, 2, 6, 5, 3, 1, 7):
        other = (me + k) % 8
        greet((near_base + other // 4, near_col + other % 4))
    for k in (2, 1, 3):
        greet(((r + 8 * k) % ROWS, c))

    wide[...] = jnp.zeros_like(wide)
    loads[0].wait()
    loads[1].wait()
    for load in loads[2:]:
        load.start()
    for k in range(K):
        for m in range(2):
            wide[k, 8 * m : 8 * m + 8, 0:32] = fac[k, m].astype(F32)
    for wave in (1, 0):
        for dest in range(4):
            word = slot_words(starts_ref, (far_col if wave else near_col) + dest)
            rows = []
            for a in range(2):
                total = None
                for b in range(4):
                    k = (word >> (4 * (4 * a + b))) & 15
                    piece = wide[k]
                    if b:
                        piece = pltpu.roll(piece, 32 * b, 1)
                    total = piece if total is None else total + piece
                rows.append(total)
            for m in range(2):
                send1[wave, m * 4 + dest] = jnp.concatenate(
                    [rows[0][8 * m : 8 * m + 8], rows[1][8 * m : 8 * m + 8]], axis=0
                ).astype(BF)
    lead = wide[0, 0:8]
    placed = lead
    for b in range(1, 4):
        placed = jnp.where(y == b, pltpu.roll(lead, 32 * b, 1), placed)
    nothing = jnp.zeros_like(placed)
    send0[...] = jnp.concatenate(
        [jnp.where(core == 0, placed, nothing), jnp.where(core == 1, placed, nothing)], axis=0
    ).astype(BF)

    def far_piece(k):
        device = (far_base + k // 4, far_col + k % 4)
        return remote(send1.at[1, k], recv1.at[1, me], sent1.at[1], came1.at[1], device)

    def far_lead(k):
        return remote(send0, recv0.at[me], sent0.at[1], came0, (far_base + 1, far_col + k))

    def near_piece(k):
        other = (me + k) % 8
        device = (near_base + other // 4, near_col + other % 4)
        return remote(send1.at[0, other], recv1.at[0, me], sent1.at[0], came1.at[0], device)

    def near_lead(k):
        sem = sent0.at[0] if k else sent0.at[2]
        return remote(send0, recv0.at[me], sem, came0, (near_base, near_col + (y + k) % 4))

    def got(ref, recv_sem):
        remote(ref, ref, load_sem.at[0], recv_sem, (sib, c)).wait_recv()

    @pl.when(far_half == 1)
    def _():
        pl.semaphore_wait(barrier, 21)
        for k in range(8):
            pl.semaphore_signal(
                far_sem,
                inc=1,
                device_id=(far_base + k // 4, far_col + k % 4),
                device_id_type=pl.DeviceIdType.MESH,
            )
        for k in range(8):
            far_piece(k).start()
        for k in range(4):
            far_lead(k).start()

    @pl.when(far_half == 0)
    def _():
        pl.semaphore_wait(barrier, 13)

    for k in range(1, 8):
        near_piece(k).start()
    pl.when(core == 1)(near_lead(0).start)
    for k in range(1, 4):
        near_lead(k).start()
    recv1[0, me] = send1[0, me]

    @pl.when(core == 0)
    def _():
        recv0[me] = send0[...]

    lane = lax.broadcasted_iota(jnp.int32, (16, 128), 1) // 32

    def unpack(wave):
        spot = far_base + core if wave else r
        turned = {}
        for s in range(2):
            for cc in range(4):
                piece = recv1[wave, s * 4 + cc].astype(F32)
                for turn in range(4):
                    turned[s, cc, turn] = pltpu.roll(piece, 32 * turn, 1) if turn else piece
        for b in range(4):
            joined = []
            for s in range(2):
                out = turned[s, 0, (0 - b) % 4]
                for cc in range(1, 4):
                    out = jnp.where(lane == cc, turned[s, cc, (cc - b) % 4], out)
                joined.append(out)
            for a in range(2):
                g_ref[wave, spot, 4 * a + b] = jnp.concatenate(
                    [joined[0][8 * a : 8 * a + 8], joined[1][8 * a : 8 * a + 8]], axis=0
                ).astype(BF)

        @pl.when(core == wave)
        def _():
            total = recv0[0].astype(F32)
            for k in range(1, 8):
                total = total + recv0[k].astype(F32)
            g_ref[wave, spot, SLOTS] = total.astype(BF)

        @pl.when(core != wave)
        def _():
            g_ref[wave, spot, SLOTS] = jnp.zeros((16, 128), BF)

    order = [
        zl,
        jnp.where(zl == 0, 1, jnp.where(zl == 1, 0, jnp.where(zl == 2, 1, 2))),
        jnp.where(zl < 2, 2, jnp.where(zl == 2, 3, 1)),
        jnp.where(zl < 2, 3, 0),
    ]
    lo, hi, whole = (0, 1, 2)
    spans = [(pl.ds(0, n), pl.ds(n, UNITS - n), pl.ds(0, UNITS)) for n in SPLITS]
    xs = [(x + k) % 4 for k in range(4)]
    zs = [(zl + k) % 4 for k in range(4)]
    nearest = (0, 1, 3, 2)

    def at(wave, xx, zz, which):
        return g_ref.at[wave, xx * 8 + (3 - zz if wave else zz) * 2 + core, spans[wave][which]]

    def send(ref, recv_sem, device, wave):
        remote(ref, ref, sent.at[wave], recv_sem, device).start()

    def along_x(wave, zz, which, recv_sem):
        for k in (1, 3, 2):
            send(at(wave, x, zz, which), recv_sem, (xs[k] * 8 + r % 8, c), wave)

    def along_z(wave, xx, which, recv_sem):
        for k in (1, 3, 2):
            send(at(wave, xx, zl, which), recv_sem, (x * 8 + zs[k] * 2 + core, c), wave)

    def across(wave, xx, zz, which):
        send(at(wave, xx, zz, which), sib_sem.at[wave], (sib, c), wave)

    def first_leg(wave):
        along_z(wave, x, lo, line_sem.at[wave, zl])
        along_x(wave, zl, hi, ring_sem.at[wave, x])
        along_x(wave, zl, lo, group_sem.at[wave, 0])
        along_z(wave, x, hi, group_sem.at[wave, 0])
        across(wave, x, zl, whole)

    def second_leg(wave):
        for i in (1, 2, 3):
            xx = xs[nearest[i]]
            got(at(wave, xx, zl, hi), ring_sem.at[wave, xx])
            along_z(wave, xx, hi, group_sem.at[wave, i])
            zz = order[i]
            got(at(wave, x, zz, lo), line_sem.at[wave, zz])
            along_x(wave, zz, lo, group_sem.at[wave, i])
            across(wave, xx, zl, hi)
            across(wave, x, zz, lo)

    def last_leg(wave):
        for i in range(4):
            got(g_ref.at[wave, pl.ds(0, 3)], group_sem.at[wave, i])
            for k in (1, 2, 3):
                across(wave, xs[nearest[k]], order[i], lo)
                across(wave, xs[nearest[i]], order[k], hi)

    got(recv1.at[0, pl.ds(0, 7)], came1.at[0])

    @pl.when(core == 0)
    def _():
        got(recv0.at[pl.ds(0, 7)], came0)

    unpack(0)
    first_leg(0)

    @pl.when(far_half == 0)
    def _():
        pl.semaphore_wait(far_sem, 8)
        for k in range(8):
            far_piece(k).start()
        for k in range(4):
            far_lead(k).start()

    second_leg(0)
    got(recv1.at[1], came1.at[1])

    @pl.when(core == 1)
    def _():
        got(recv0, came0)

    unpack(1)
    first_leg(1)

    second_leg(1)
    last_leg(0)
    last_leg(1)

    for wave in range(2):
        got(g_ref.at[wave, pl.ds(0, 16)], sib_sem.at[wave])

    def left(ref, send_sem):
        remote(ref, ref, send_sem, load_sem.at[0], (sib, c)).wait_send()

    for wave in range(2):
        left(g_ref.at[wave, pl.ds(0, 31)], sent.at[wave])
    left(send1.at[0, pl.ds(0, 7)], sent1.at[0])
    left(send1.at[1], sent1.at[1])
    left(recv0.at[pl.ds(0, 3)], sent0.at[0])
    left(recv0.at[pl.ds(0, 4)], sent0.at[1])
    pl.when(core == 1)(near_lead(0).wait_send)
    for load in loads[2:]:
        load.wait()


def early():
    r, c = lax.axis_index("row"), lax.axis_index("col")
    return jnp.logical_and(c < 4, 2 * (r // 8) + 2 * c + 3 * ((r // 2) % 4) <= EARLY)


def copy_kernel(q, z, q_out, z_out, held, in_sem, out_sem):
    @pl.when(early())
    def _():
        ins, outs = [], []
        for i in range(PARTS):
            part = pl.ds(128 // PARTS * i, 128 // PARTS)
            for n, (src, dst) in enumerate(((q, q_out), (z, z_out))):
                spot = 2 * i + n
                ins.append(pltpu.make_async_copy(src.at[part], held.at[n, part], in_sem.at[spot]))
                outs.append(pltpu.make_async_copy(held.at[n, part], dst.at[part], out_sem.at[spot]))
        for copy in ins:
            copy.start()
        for arrive, leave in zip(ins, outs):
            arrive.wait()
            leave.start()
        for copy in outs:
            copy.wait()


def apply_kernel(
    starts, flags, q, z, s, t, g, q_copied, z_copied, q_out, z_out, s_out, t_out, q_new, z_new, band, q_sem, z_sem, b_sem, whole_sem
):
    r = lax.axis_index("row")
    c = lax.axis_index("col")
    word = slot_words(starts, c)
    count = jnp.int32(0)
    windows = jnp.int32(0)
    for k in range(K):
        mine = (starts[k] >> 13) == c
        count = count + jnp.where(mine, 1, 0)
        bit = jnp.left_shift(jnp.int32(1), (starts[k] >> 8) & (TILES - 1))
        windows = jnp.where(jnp.logical_and(mine, flags[k] == 1), windows | bit, windows)

    wholes = [pltpu.make_async_copy(q, q_out, whole_sem.at[0]), pltpu.make_async_copy(z, z_out, whole_sem.at[1])]
    for whole in wholes:
        pl.when(jnp.logical_not(early()))(whole.start)

    def q_copy(j, tile):
        return pltpu.make_async_copy(q_new.at[j], q_out.at[:, pl.ds(pl.multiple_of(tile * W, W), W)], q_sem.at[j])

    def z_copy(j, tile):
        return pltpu.make_async_copy(z_new.at[j], z_out.at[:, pl.ds(pl.multiple_of(tile * W, W), W)], z_sem.at[j])

    far_half = c // 4

    def factor(side, slot):
        parts = [g[h ^ far_half, :, side, slot].reshape(W, W // 2) for h in range(2)]
        return jnp.concatenate(parts, axis=1)

    band_slot = jnp.int32(0)
    slots = []
    for j in range(SLOTS):
        k = (word >> (4 * j)) & 15
        tile = (starts[k] >> 8) & (TILES - 1)
        live = jnp.logical_and(j < count, flags[k] == 1)
        band_slot = jnp.where(jnp.logical_and(j < count, tile == r), j, band_slot)
        slots.append((live, tile))

        @pl.when(live)
        def _():
            where = pl.ds(pl.multiple_of(tile * W, W), W)
            q_new[j] = jnp.dot(q[:, where], factor(0, j), preferred_element_type=F32).astype(BF)
            z_new[j] = jnp.dot(z[:, where], factor(1, j), preferred_element_type=F32).astype(BF)

    band_live = ((windows >> r) & 1) == 1
    right = factor(1, band_slot)
    lead = jnp.concatenate(
        [g[h ^ far_half, :, h ^ far_half, SLOTS].reshape(W, W // 2) for h in range(2)], axis=1
    )
    outs = []
    for i, (ref, out) in enumerate(((s, s_out), (t, t_out))):
        fresh = jnp.dot(ref[...], right, preferred_element_type=F32).astype(BF)
        mid = jnp.where(band_live, fresh, ref[...])
        band[i] = lax.dot_general(
            lead, mid, (((0,), (0,)), ((), ())), preferred_element_type=F32
        ).astype(BF)
        copy = pltpu.make_async_copy(band.at[i], out, b_sem.at[i])
        copy.start()
        outs.append(copy)
    for whole in wholes:
        pl.when(jnp.logical_not(early()))(whole.wait)
    for j, (live, tile) in enumerate(slots):

        @pl.when(live)
        def _():
            q_copy(j, tile).start()
            z_copy(j, tile).start()

    for copy in outs:
        copy.wait()
    for j, (live, tile) in enumerate(slots):

        @pl.when(live)
        def _():
            q_copy(j, tile).wait()
            z_copy(j, tile).wait()


def local(s_band, t_band, q_rows, z_rows, factors, starts, flags):
    anywhere = pl.BlockSpec(memory_space=pl.ANY)
    hbm = pl.BlockSpec(memory_space=pltpu.HBM)
    vmem = pl.BlockSpec(memory_space=pltpu.VMEM)
    smem = pl.BlockSpec(memory_space=pltpu.SMEM)
    dma = pltpu.SemaphoreType.DMA
    copied = pl.pallas_call(
        copy_kernel,
        out_shape=(
            jax.ShapeDtypeStruct(q_rows.shape, BF),
            jax.ShapeDtypeStruct(z_rows.shape, BF),
        ),
        in_specs=[hbm] * 2,
        out_specs=[hbm] * 2,
        scratch_shapes=[pltpu.VMEM((2, *q_rows.shape), BF), dma((2 * PARTS,)), dma((2 * PARTS,))],
        compiler_params=pltpu.CompilerParams(vmem_limit_bytes=32 << 20),
    )(*(pltpu.with_memory_space_constraint(a, pltpu.HBM) for a in (q_rows, z_rows)))
    gathered, qv, zv, sv, tv = pl.pallas_call(
        gather_kernel,
        out_shape=(
            pltpu.VMEM((2, ROWS, UNITS, 16, 128), BF),
            pltpu.VMEM(q_rows.shape, BF),
            pltpu.VMEM(z_rows.shape, BF),
            pltpu.VMEM(s_band.shape, BF),
            pltpu.VMEM(t_band.shape, BF),
        ),
        in_specs=[hbm] * 8,
        out_specs=[vmem] * 5,
        scratch_shapes=[
            pltpu.SMEM((K,), jnp.int32),
            pltpu.VMEM((K, 2, 8, 32), BF),
            pltpu.VMEM((K, 16, 128), F32),
            pltpu.VMEM((2, 8, 16, 128), BF),
            pltpu.VMEM((2, 8, 16, 128), BF),
            pltpu.VMEM((16, 128), BF),
            pltpu.VMEM((8, 16, 128), BF),
            dma((6,)),
            dma((2,)), dma((3,)), dma((2,)), dma(()),
            dma((2,)), dma((2, 4)), dma((2, 4)), dma((2, 4)), dma((2,)),
            pltpu.SemaphoreType.REGULAR,
        ],
        compiler_params=pltpu.CompilerParams(
            collective_id=0, has_side_effects=True, vmem_limit_bytes=32 << 20
        ),
    )(*(pltpu.with_memory_space_constraint(a, pltpu.HBM) for a in (starts, factors, q_rows, z_rows, s_band, t_band, *copied)))
    gathered = gathered.reshape(2, 16, 2, UNITS, 16, 128)
    pin = lambda a: pltpu.with_memory_space_constraint(a, pltpu.VMEM)
    return tuple(
        pl.pallas_call(
            apply_kernel,
            out_shape=(
                jax.ShapeDtypeStruct(q_rows.shape, BF),
                jax.ShapeDtypeStruct(z_rows.shape, BF),
                jax.ShapeDtypeStruct(s_band.shape, BF),
                jax.ShapeDtypeStruct(t_band.shape, BF),
            ),
            in_specs=[smem, smem] + [vmem] * 5 + [hbm] * 2,
            out_specs=[hbm] * 2 + [anywhere] * 2,
            input_output_aliases={7: 0, 8: 1},
            scratch_shapes=[
                pltpu.VMEM((SLOTS, 128, W), BF),
                pltpu.VMEM((SLOTS, 128, W), BF),
                pltpu.VMEM((2, W, W), BF),
                dma((SLOTS,)),
                dma((SLOTS,)),
                dma((2,)),
                dma((2,)),
            ],
            compiler_params=pltpu.CompilerParams(vmem_limit_bytes=32 << 20),
        )(starts, flags, *(pin(a) for a in (qv, zv, sv, tv, gathered)), *(pltpu.with_memory_space_constraint(a, pltpu.HBM) for a in copied))
    )


def solution(mesh):
    in_specs = (
        P(None, ("col", "row")),
        P(None, ("col", "row")),
        P("row", "col"),
        P("row", "col"),
        P(None, None, "row", "col"),
        P(),
        P(),
    )
    out_specs = (P("row", "col"), P("row", "col"), P(None, ("col", "row")), P(None, ("col", "row")))
    return jax.shard_map(local, mesh=mesh, in_specs=in_specs, out_specs=out_specs, check_vma=False)
```

```python
import jax
import jax.numpy as jnp
from jax import lax
from jax.experimental import pallas as pl
from jax.experimental.pallas import tpu as pltpu
from jax.sharding import PartitionSpec as P

W = 256
K = 16
SLOTS = 8
UNITS = SLOTS + 1
ROWS = 32
COLS = 8
TILES = 32
SPLITS = (7, 5)
EARLY = 2
PARTS = 4
BF = jnp.bfloat16
F32 = jnp.float32


def slot_words(starts_ref, column):
    word = jnp.int32(0)
    for k in reversed(range(K)):
        mine = (starts_ref[k] >> 13) == column
        word = jnp.where(mine, (word << 4) | k, word)
    return word


def remote(src, dst, send_sem, recv_sem, device):
    return pltpu.make_async_remote_copy(
        src_ref=src,
        dst_ref=dst,
        send_sem=send_sem,
        recv_sem=recv_sem,
        device_id=device,
        device_id_type=pl.DeviceIdType.MESH,
    )


def gather_kernel(
    starts_hbm, flags_hbm, factors_hbm, q_hbm, z_hbm, s_hbm, t_hbm, q_copied, z_copied,
    g_ref, qv, zv, sv, tv, starts_ref, flags_ref,
    fac, wide, send1, recv1, send0, recv0,
    load_sem, sent1, sent0, came1, came0, sent, line_sem, ring_sem, group_sem, sib_sem, far_sem,
):
    r = lax.axis_index("row")
    c = lax.axis_index("col")
    core = r % 2
    x = r // 8
    zl = (r // 2) % 4
    far_half = c // 4
    y = c % 4
    me = core * 4 + y
    sib = r + 1 - 2 * core
    near_base = r - core
    far_base = x * 8 + (3 - zl) * 2
    near_col = far_half * 4
    far_col = (1 - far_half) * 4

    barrier = pltpu.get_barrier_semaphore()

    def greet(device):
        pl.semaphore_signal(barrier, inc=1, device_id=device, device_id_type=pl.DeviceIdType.MESH)

    loads = [
        pltpu.make_async_copy(a, b, load_sem.at[i])
        for i, (a, b) in enumerate(
            [(factors_hbm, fac), (starts_hbm, starts_ref), (q_hbm, qv), (z_hbm, zv), (s_hbm, sv), (t_hbm, tv), (flags_hbm, flags_ref)]
        )
    ]
    loads[0].start()
    loads[1].start()

    @pl.when(far_half == 0)
    def _():
        for k in range(8):
            greet((far_base + k // 4, far_col + k % 4))

    for k in (3, 1, 2):
        greet((x * 8 + (zl + k) % 4 * 2 + core, c))
    for k in (4, 2, 6, 5, 3, 1, 7):
        other = (me + k) % 8
        greet((near_base + other // 4, near_col + other % 4))
    for k in (2, 1, 3):
        greet(((r + 8 * k) % ROWS, c))

    wide[...] = jnp.zeros_like(wide)
    loads[0].wait()
    loads[1].wait()
    for load in loads[2:]:
        load.start()
    for k in range(K):
        for m in range(2):
            wide[k, 8 * m : 8 * m + 8, 0:32] = fac[k, m].astype(F32)
    for wave in (1, 0):
        for dest in range(4):
            word = slot_words(starts_ref, (far_col if wave else near_col) + dest)
            rows = []
            for a in range(2):
                total = None
                for b in range(4):
                    k = (word >> (4 * (4 * a + b))) & 15
                    piece = wide[k]
                    if b:
                        piece = pltpu.roll(piece, 32 * b, 1)
                    total = piece if total is None else total + piece
                rows.append(total)
            for m in range(2):
                send1[wave, m * 4 + dest] = jnp.concatenate(
                    [rows[0][8 * m : 8 * m + 8], rows[1][8 * m : 8 * m + 8]], axis=0
                ).astype(BF)
    lead = wide[0, 0:8]
    placed = lead
    for b in range(1, 4):
        placed = jnp.where(y == b, pltpu.roll(lead, 32 * b, 1), placed)
    nothing = jnp.zeros_like(placed)
    send0[...] = jnp.concatenate(
        [jnp.where(core == 0, placed, nothing), jnp.where(core == 1, placed, nothing)], axis=0
    ).astype(BF)

    def far_piece(k):
        device = (far_base + k // 4, far_col + k % 4)
        return remote(send1.at[1, k], recv1.at[1, me], sent1.at[1], came1.at[1], device)

    def far_lead(k):
        return remote(send0, recv0.at[me], sent0.at[1], came0, (far_base + 1, far_col + k))

    def near_piece(k):
        other = (me + k) % 8
        device = (near_base + other // 4, near_col + other % 4)
        return remote(send1.at[0, other], recv1.at[0, me], sent1.at[0], came1.at[0], device)

    def near_lead(k):
        sem = sent0.at[0] if k else sent0.at[2]
        return remote(send0, recv0.at[me], sem, came0, (near_base, near_col + (y + k) % 4))

    def got(ref, recv_sem):
        remote(ref, ref, load_sem.at[0], recv_sem, (sib, c)).wait_recv()

    @pl.when(far_half == 1)
    def _():
        pl.semaphore_wait(barrier, 21)
        for k in range(8):
            pl.semaphore_signal(
                far_sem,
                inc=1,
                device_id=(far_base + k // 4, far_col + k % 4),
                device_id_type=pl.DeviceIdType.MESH,
            )
        for k in range(8):
            far_piece(k).start()
        for k in range(4):
            far_lead(k).start()

    @pl.when(far_half == 0)
    def _():
        pl.semaphore_wait(barrier, 13)

    for k in range(1, 8):
        near_piece(k).start()
    pl.when(core == 1)(near_lead(0).start)
    for k in range(1, 4):
        near_lead(k).start()
    recv1[0, me] = send1[0, me]

    @pl.when(core == 0)
    def _():
        recv0[me] = send0[...]

    lane = lax.broadcasted_iota(jnp.int32, (16, 128), 1) // 32

    def unpack(wave):
        spot = far_base + core if wave else r
        turned = {}
        for s in range(2):
            for cc in range(4):
                piece = recv1[wave, s * 4 + cc].astype(F32)
                for turn in range(4):
                    turned[s, cc, turn] = pltpu.roll(piece, 32 * turn, 1) if turn else piece
        for b in range(4):
            joined = []
            for s in range(2):
                out = turned[s, 0, (0 - b) % 4]
                for cc in range(1, 4):
                    out = jnp.where(lane == cc, turned[s, cc, (cc - b) % 4], out)
                joined.append(out)
            for a in range(2):
                g_ref[wave, spot, 4 * a + b] = jnp.concatenate(
                    [joined[0][8 * a : 8 * a + 8], joined[1][8 * a : 8 * a + 8]], axis=0
                ).astype(BF)

        @pl.when(core == wave)
        def _():
            total = recv0[0].astype(F32)
            for k in range(1, 8):
                total = total + recv0[k].astype(F32)
            g_ref[wave, spot, SLOTS] = total.astype(BF)

        @pl.when(core != wave)
        def _():
            g_ref[wave, spot, SLOTS] = jnp.zeros((16, 128), BF)

    order = [
        zl,
        jnp.where(zl == 0, 1, jnp.where(zl == 1, 0, jnp.where(zl == 2, 1, 2))),
        jnp.where(zl < 2, 2, jnp.where(zl == 2, 3, 1)),
        jnp.where(zl < 2, 3, 0),
    ]
    lo, hi, whole = (0, 1, 2)
    spans = [(pl.ds(0, n), pl.ds(n, UNITS - n), pl.ds(0, UNITS)) for n in SPLITS]
    xs = [(x + k) % 4 for k in range(4)]
    zs = [(zl + k) % 4 for k in range(4)]
    nearest = (0, 1, 3, 2)

    def at(wave, xx, zz, which):
        return g_ref.at[wave, xx * 8 + (3 - zz if wave else zz) * 2 + core, spans[wave][which]]

    def send(ref, recv_sem, device, wave):
        remote(ref, ref, sent.at[wave], recv_sem, device).start()

    def along_x(wave, zz, which, recv_sem):
        for k in (1, 3, 2):
            send(at(wave, x, zz, which), recv_sem, (xs[k] * 8 + r % 8, c), wave)

    def along_z(wave, xx, which, recv_sem):
        for k in (1, 3, 2):
            send(at(wave, xx, zl, which), recv_sem, (x * 8 + zs[k] * 2 + core, c), wave)

    def across(wave, xx, zz, which):
        send(at(wave, xx, zz, which), sib_sem.at[wave], (sib, c), wave)

    def first_leg(wave):
        along_z(wave, x, lo, line_sem.at[wave, zl])
        along_x(wave, zl, hi, ring_sem.at[wave, x])
        along_x(wave, zl, lo, group_sem.at[wave, 0])
        along_z(wave, x, hi, group_sem.at[wave, 0])
        across(wave, x, zl, whole)

    def second_leg(wave):
        for i in (1, 2, 3):
            xx = xs[nearest[i]]
            got(at(wave, xx, zl, hi), ring_sem.at[wave, xx])
            along_z(wave, xx, hi, group_sem.at[wave, i])
            zz = order[i]
            got(at(wave, x, zz, lo), line_sem.at[wave, zz])
            along_x(wave, zz, lo, group_sem.at[wave, i])
            across(wave, xx, zl, hi)
            across(wave, x, zz, lo)

    def last_leg(wave):
        for i in range(4):
            got(g_ref.at[wave, pl.ds(0, 3)], group_sem.at[wave, i])
            for k in (1, 2, 3):
                across(wave, xs[nearest[k]], order[i], lo)
                across(wave, xs[nearest[i]], order[k], hi)

    got(recv1.at[0, pl.ds(0, 7)], came1.at[0])

    @pl.when(core == 0)
    def _():
        got(recv0.at[pl.ds(0, 7)], came0)

    unpack(0)
    first_leg(0)

    @pl.when(far_half == 0)
    def _():
        pl.semaphore_wait(far_sem, 8)
        for k in range(8):
            far_piece(k).start()
        for k in range(4):
            far_lead(k).start()

    second_leg(0)
    got(recv1.at[1], came1.at[1])

    @pl.when(core == 1)
    def _():
        got(recv0, came0)

    unpack(1)
    first_leg(1)

    second_leg(1)
    last_leg(0)
    last_leg(1)

    for wave in range(2):
        got(g_ref.at[wave, pl.ds(0, 16)], sib_sem.at[wave])

    def left(ref, send_sem):
        remote(ref, ref, send_sem, load_sem.at[0], (sib, c)).wait_send()

    for wave in range(2):
        left(g_ref.at[wave, pl.ds(0, 31)], sent.at[wave])
    left(send1.at[0, pl.ds(0, 7)], sent1.at[0])
    left(send1.at[1], sent1.at[1])
    left(recv0.at[pl.ds(0, 3)], sent0.at[0])
    left(recv0.at[pl.ds(0, 4)], sent0.at[1])
    pl.when(core == 1)(near_lead(0).wait_send)
    for load in loads[2:]:
        load.wait()


def early():
    r, c = lax.axis_index("row"), lax.axis_index("col")
    return jnp.logical_and(c < 4, 2 * (r // 8) + 2 * c + 3 * ((r // 2) % 4) <= EARLY)


def copy_kernel(q, z, q_out, z_out, held, in_sem, out_sem):
    @pl.when(early())
    def _():
        ins, outs = [], []
        for i in range(PARTS):
            part = pl.ds(128 // PARTS * i, 128 // PARTS)
            for n, (src, dst) in enumerate(((q, q_out), (z, z_out))):
                spot = 2 * i + n
                ins.append(pltpu.make_async_copy(src.at[part], held.at[n, part], in_sem.at[spot]))
                outs.append(pltpu.make_async_copy(held.at[n, part], dst.at[part], out_sem.at[spot]))
        for copy in ins:
            copy.start()
        for arrive, leave in zip(ins, outs):
            arrive.wait()
            leave.start()
        for copy in outs:
            copy.wait()


def apply_kernel(
    starts, flags, q, z, s, t, g, q_copied, z_copied, q_out, z_out, s_out, t_out, q_new, z_new, band, q_sem, z_sem, b_sem, whole_sem
):
    r = lax.axis_index("row")
    c = lax.axis_index("col")
    wholes = [pltpu.make_async_copy(q, q_out, whole_sem.at[0]), pltpu.make_async_copy(z, z_out, whole_sem.at[1])]
    for whole in wholes:
        pl.when(jnp.logical_not(early()))(whole.start)

    word = slot_words(starts, c)
    count = jnp.int32(0)
    windows = jnp.int32(0)
    for k in range(K):
        mine = (starts[k] >> 13) == c
        count = count + jnp.where(mine, 1, 0)
        bit = jnp.left_shift(jnp.int32(1), (starts[k] >> 8) & (TILES - 1))
        windows = jnp.where(jnp.logical_and(mine, flags[k] == 1), windows | bit, windows)

    def q_copy(j, tile):
        return pltpu.make_async_copy(q_new.at[j], q_out.at[:, pl.ds(pl.multiple_of(tile * W, W), W)], q_sem.at[j])

    def z_copy(j, tile):
        return pltpu.make_async_copy(z_new.at[j], z_out.at[:, pl.ds(pl.multiple_of(tile * W, W), W)], z_sem.at[j])

    far_half = c // 4

    def factor(side, slot):
        parts = [g[h ^ far_half, :, side, slot].reshape(W, W // 2) for h in range(2)]
        return jnp.concatenate(parts, axis=1)

    band_slot = jnp.int32(0)
    slots = []
    for j in range(SLOTS):
        k = (word >> (4 * j)) & 15
        tile = (starts[k] >> 8) & (TILES - 1)
        live = jnp.logical_and(j < count, flags[k] == 1)
        band_slot = jnp.where(jnp.logical_and(j < count, tile == r), j, band_slot)
        slots.append((live, tile))

        @pl.when(live)
        def _():
            where = pl.ds(pl.multiple_of(tile * W, W), W)
            q_new[j] = jnp.dot(q[:, where], factor(0, j), preferred_element_type=F32).astype(BF)
            z_new[j] = jnp.dot(z[:, where], factor(1, j), preferred_element_type=F32).astype(BF)

    band_live = ((windows >> r) & 1) == 1
    right = factor(1, band_slot)
    lead = jnp.concatenate(
        [g[h ^ far_half, :, h ^ far_half, SLOTS].reshape(W, W // 2) for h in range(2)], axis=1
    )
    outs = []
    for i, (ref, out) in enumerate(((s, s_out), (t, t_out))):
        fresh = jnp.dot(ref[...], right, preferred_element_type=F32).astype(BF)
        mid = jnp.where(band_live, fresh, ref[...])
        band[i] = lax.dot_general(
            lead, mid, (((0,), (0,)), ((), ())), preferred_element_type=F32
        ).astype(BF)
        copy = pltpu.make_async_copy(band.at[i], out, b_sem.at[i])
        copy.start()
        outs.append(copy)
    for whole, new_copy in zip(wholes, (q_copy, z_copy)):
        pl.when(jnp.logical_not(early()))(whole.wait)
        for j, (live, tile) in enumerate(slots):
            pl.when(live)(new_copy(j, tile).start)

    for copy in outs:
        copy.wait()
    for j, (live, tile) in enumerate(slots):

        @pl.when(live)
        def _():
            q_copy(j, tile).wait()
            z_copy(j, tile).wait()


def local(s_band, t_band, q_rows, z_rows, factors, starts, flags):
    anywhere = pl.BlockSpec(memory_space=pl.ANY)
    hbm = pl.BlockSpec(memory_space=pltpu.HBM)
    vmem = pl.BlockSpec(memory_space=pltpu.VMEM)
    smem = pl.BlockSpec(memory_space=pltpu.SMEM)
    dma = pltpu.SemaphoreType.DMA
    copied = pl.pallas_call(
        copy_kernel,
        out_shape=(
            jax.ShapeDtypeStruct(q_rows.shape, BF),
            jax.ShapeDtypeStruct(z_rows.shape, BF),
        ),
        in_specs=[hbm] * 2,
        out_specs=[hbm] * 2,
        scratch_shapes=[pltpu.VMEM((2, *q_rows.shape), BF), dma((2 * PARTS,)), dma((2 * PARTS,))],
        compiler_params=pltpu.CompilerParams(vmem_limit_bytes=32 << 20),
    )(*(pltpu.with_memory_space_constraint(a, pltpu.HBM) for a in (q_rows, z_rows)))
    gathered, qv, zv, sv, tv, starts_held, flags_held = pl.pallas_call(
        gather_kernel,
        out_shape=(
            pltpu.VMEM((2, ROWS, UNITS, 16, 128), BF),
            pltpu.VMEM(q_rows.shape, BF),
            pltpu.VMEM(z_rows.shape, BF),
            pltpu.VMEM(s_band.shape, BF),
            pltpu.VMEM(t_band.shape, BF),
            pltpu.SMEM((K,), jnp.int32),
            pltpu.SMEM((K,), jnp.int32),
        ),
        in_specs=[hbm] * 9,
        out_specs=[vmem] * 5 + [smem] * 2,
        scratch_shapes=[
            pltpu.VMEM((K, 2, 8, 32), BF),
            pltpu.VMEM((K, 16, 128), F32),
            pltpu.VMEM((2, 8, 16, 128), BF),
            pltpu.VMEM((2, 8, 16, 128), BF),
            pltpu.VMEM((16, 128), BF),
            pltpu.VMEM((8, 16, 128), BF),
            dma((7,)),
            dma((2,)), dma((3,)), dma((2,)), dma(()),
            dma((2,)), dma((2, 4)), dma((2, 4)), dma((2, 4)), dma((2,)),
            pltpu.SemaphoreType.REGULAR,
        ],
        compiler_params=pltpu.CompilerParams(
            collective_id=0, has_side_effects=True, vmem_limit_bytes=32 << 20
        ),
    )(*(pltpu.with_memory_space_constraint(a, pltpu.HBM) for a in (starts, flags, factors, q_rows, z_rows, s_band, t_band, *copied)))
    gathered = gathered.reshape(2, 16, 2, UNITS, 16, 128)
    pin = lambda a: pltpu.with_memory_space_constraint(a, pltpu.VMEM)
    return tuple(
        pl.pallas_call(
            apply_kernel,
            out_shape=(
                jax.ShapeDtypeStruct(q_rows.shape, BF),
                jax.ShapeDtypeStruct(z_rows.shape, BF),
                jax.ShapeDtypeStruct(s_band.shape, BF),
                jax.ShapeDtypeStruct(t_band.shape, BF),
            ),
            in_specs=[smem, smem] + [vmem] * 5 + [hbm] * 2,
            out_specs=[hbm] * 2 + [anywhere] * 2,
            input_output_aliases={7: 0, 8: 1},
            scratch_shapes=[
                pltpu.VMEM((SLOTS, 128, W), BF),
                pltpu.VMEM((SLOTS, 128, W), BF),
                pltpu.VMEM((2, W, W), BF),
                dma((SLOTS,)),
                dma((SLOTS,)),
                dma((2,)),
                dma((2,)),
            ],
            compiler_params=pltpu.CompilerParams(vmem_limit_bytes=32 << 20),
        )(*(pltpu.with_memory_space_constraint(a, pltpu.SMEM) for a in (starts_held, flags_held)), *(pin(a) for a in (qv, zv, sv, tv, gathered)), *(pltpu.with_memory_space_constraint(a, pltpu.HBM) for a in copied))
    )


def solution(mesh):
    in_specs = (
        P(None, ("col", "row")),
        P(None, ("col", "row")),
        P("row", "col"),
        P("row", "col"),
        P(None, None, "row", "col"),
        P(),
        P(),
    )
    out_specs = (P("row", "col"), P("row", "col"), P(None, ("col", "row")), P(None, ("col", "row")))
    return jax.shard_map(local, mesh=mesh, in_specs=in_specs, out_specs=out_specs, check_vma=False)
```

```python
import jax
import jax.numpy as jnp
from jax import lax
from jax.experimental import pallas as pl
from jax.experimental.pallas import tpu as pltpu
from jax.sharding import PartitionSpec as P

W = 256
K = 16
SLOTS = 8
UNITS = SLOTS + 1
ROWS = 32
COLS = 8
TILES = 32
SPLITS = (7, 5)
EARLY = 4
PARTS = 4
BF = jnp.bfloat16
F32 = jnp.float32


def slot_words(starts_ref, column):
    word = jnp.int32(0)
    for k in reversed(range(K)):
        mine = (starts_ref[k] >> 13) == column
        word = jnp.where(mine, (word << 4) | k, word)
    return word


def remote(src, dst, send_sem, recv_sem, device):
    return pltpu.make_async_remote_copy(
        src_ref=src,
        dst_ref=dst,
        send_sem=send_sem,
        recv_sem=recv_sem,
        device_id=device,
        device_id_type=pl.DeviceIdType.MESH,
    )


def gather_kernel(
    starts_hbm, flags_hbm, factors_hbm, q_hbm, z_hbm, s_hbm, t_hbm, q_copied, z_copied,
    g_ref, qv, zv, sv, tv, starts_ref, flags_ref,
    fac, wide, send1, recv1, send0, recv0,
    load_sem, sent1, sent0, came1, came0, sent, line_sem, ring_sem, group_sem, sib_sem, far_sem,
):
    r = lax.axis_index("row")
    c = lax.axis_index("col")
    core = r % 2
    x = r // 8
    zl = (r // 2) % 4
    far_half = c // 4
    y = c % 4
    me = core * 4 + y
    sib = r + 1 - 2 * core
    near_base = r - core
    far_base = x * 8 + (3 - zl) * 2
    near_col = far_half * 4
    far_col = (1 - far_half) * 4

    barrier = pltpu.get_barrier_semaphore()

    def greet(device):
        pl.semaphore_signal(barrier, inc=1, device_id=device, device_id_type=pl.DeviceIdType.MESH)

    loads = [
        pltpu.make_async_copy(a, b, load_sem.at[i])
        for i, (a, b) in enumerate(
            [(factors_hbm, fac), (starts_hbm, starts_ref), (q_hbm, qv), (z_hbm, zv), (s_hbm, sv), (t_hbm, tv), (flags_hbm, flags_ref)]
        )
    ]
    loads[0].start()
    loads[1].start()

    @pl.when(far_half == 0)
    def _():
        for k in range(8):
            greet((far_base + k // 4, far_col + k % 4))

    for k in (3, 1, 2):
        greet((x * 8 + (zl + k) % 4 * 2 + core, c))
    for k in (4, 2, 6, 5, 3, 1, 7):
        other = (me + k) % 8
        greet((near_base + other // 4, near_col + other % 4))
    for k in (2, 1, 3):
        greet(((r + 8 * k) % ROWS, c))

    wide[...] = jnp.zeros_like(wide)
    loads[0].wait()
    loads[1].wait()
    for load in loads[2:]:
        load.start()
    for k in range(K):
        for m in range(2):
            wide[k, 8 * m : 8 * m + 8, 0:32] = fac[k, m].astype(F32)
    for wave in (1, 0):
        for dest in range(4):
            word = slot_words(starts_ref, (far_col if wave else near_col) + dest)
            rows = []
            for a in range(2):
                total = None
                for b in range(4):
                    k = (word >> (4 * (4 * a + b))) & 15
                    piece = wide[k]
                    if b:
                        piece = pltpu.roll(piece, 32 * b, 1)
                    total = piece if total is None else total + piece
                rows.append(total)
            for m in range(2):
                send1[wave, m * 4 + dest] = jnp.concatenate(
                    [rows[0][8 * m : 8 * m + 8], rows[1][8 * m : 8 * m + 8]], axis=0
                ).astype(BF)
    lead = wide[0, 0:8]
    placed = lead
    for b in range(1, 4):
        placed = jnp.where(y == b, pltpu.roll(lead, 32 * b, 1), placed)
    nothing = jnp.zeros_like(placed)
    send0[...] = jnp.concatenate(
        [jnp.where(core == 0, placed, nothing), jnp.where(core == 1, placed, nothing)], axis=0
    ).astype(BF)

    def far_piece(k):
        device = (far_base + k // 4, far_col + k % 4)
        return remote(send1.at[1, k], recv1.at[1, me], sent1.at[1], came1.at[1], device)

    def far_lead(k):
        return remote(send0, recv0.at[me], sent0.at[1], came0, (far_base + 1, far_col + k))

    def near_piece(k):
        other = (me + k) % 8
        device = (near_base + other // 4, near_col + other % 4)
        return remote(send1.at[0, other], recv1.at[0, me], sent1.at[0], came1.at[0], device)

    def near_lead(k):
        sem = sent0.at[0] if k else sent0.at[2]
        return remote(send0, recv0.at[me], sem, came0, (near_base, near_col + (y + k) % 4))

    def got(ref, recv_sem):
        remote(ref, ref, load_sem.at[0], recv_sem, (sib, c)).wait_recv()

    @pl.when(far_half == 1)
    def _():
        pl.semaphore_wait(barrier, 21)
        for k in range(8):
            pl.semaphore_signal(
                far_sem,
                inc=1,
                device_id=(far_base + k // 4, far_col + k % 4),
                device_id_type=pl.DeviceIdType.MESH,
            )
        for k in range(8):
            far_piece(k).start()
        for k in range(4):
            far_lead(k).start()

    @pl.when(far_half == 0)
    def _():
        pl.semaphore_wait(barrier, 13)

    for k in range(1, 8):
        near_piece(k).start()
    pl.when(core == 1)(near_lead(0).start)
    for k in range(1, 4):
        near_lead(k).start()
    recv1[0, me] = send1[0, me]

    @pl.when(core == 0)
    def _():
        recv0[me] = send0[...]

    lane = lax.broadcasted_iota(jnp.int32, (16, 128), 1) // 32

    def unpack(wave):
        spot = far_base + core if wave else r
        turned = {}
        for s in range(2):
            for cc in range(4):
                piece = recv1[wave, s * 4 + cc].astype(F32)
                for turn in range(4):
                    turned[s, cc, turn] = pltpu.roll(piece, 32 * turn, 1) if turn else piece
        for b in range(4):
            joined = []
            for s in range(2):
                out = turned[s, 0, (0 - b) % 4]
                for cc in range(1, 4):
                    out = jnp.where(lane == cc, turned[s, cc, (cc - b) % 4], out)
                joined.append(out)
            for a in range(2):
                g_ref[wave, spot, 4 * a + b] = jnp.concatenate(
                    [joined[0][8 * a : 8 * a + 8], joined[1][8 * a : 8 * a + 8]], axis=0
                ).astype(BF)

        @pl.when(core == wave)
        def _():
            total = recv0[0].astype(F32)
            for k in range(1, 8):
                total = total + recv0[k].astype(F32)
            g_ref[wave, spot, SLOTS] = total.astype(BF)

        @pl.when(core != wave)
        def _():
            g_ref[wave, spot, SLOTS] = jnp.zeros((16, 128), BF)

    order = [
        zl,
        jnp.where(zl == 0, 1, jnp.where(zl == 1, 0, jnp.where(zl == 2, 1, 2))),
        jnp.where(zl < 2, 2, jnp.where(zl == 2, 3, 1)),
        jnp.where(zl < 2, 3, 0),
    ]
    lo, hi, whole = (0, 1, 2)
    spans = [(pl.ds(0, n), pl.ds(n, UNITS - n), pl.ds(0, UNITS)) for n in SPLITS]
    xs = [(x + k) % 4 for k in range(4)]
    zs = [(zl + k) % 4 for k in range(4)]
    nearest = (0, 1, 3, 2)

    def at(wave, xx, zz, which):
        return g_ref.at[wave, xx * 8 + (3 - zz if wave else zz) * 2 + core, spans[wave][which]]

    def send(ref, recv_sem, device, wave):
        remote(ref, ref, sent.at[wave], recv_sem, device).start()

    def along_x(wave, zz, which, recv_sem):
        for k in (1, 3, 2):
            send(at(wave, x, zz, which), recv_sem, (xs[k] * 8 + r % 8, c), wave)

    def along_z(wave, xx, which, recv_sem):
        for k in (1, 3, 2):
            send(at(wave, xx, zl, which), recv_sem, (x * 8 + zs[k] * 2 + core, c), wave)

    def across(wave, xx, zz, which):
        send(at(wave, xx, zz, which), sib_sem.at[wave], (sib, c), wave)

    def first_leg(wave):
        along_z(wave, x, lo, line_sem.at[wave, zl])
        along_x(wave, zl, hi, ring_sem.at[wave, x])
        along_x(wave, zl, lo, group_sem.at[wave, 0])
        along_z(wave, x, hi, group_sem.at[wave, 0])
        across(wave, x, zl, whole)

    def second_leg(wave):
        for i in (1, 2, 3):
            xx = xs[nearest[i]]
            got(at(wave, xx, zl, hi), ring_sem.at[wave, xx])
            along_z(wave, xx, hi, group_sem.at[wave, i])
            zz = order[i]
            got(at(wave, x, zz, lo), line_sem.at[wave, zz])
            along_x(wave, zz, lo, group_sem.at[wave, i])
            across(wave, xx, zl, hi)
            across(wave, x, zz, lo)

    def last_leg(wave):
        for i in range(4):
            got(g_ref.at[wave, pl.ds(0, 3)], group_sem.at[wave, i])
            for k in (1, 2, 3):
                across(wave, xs[nearest[k]], order[i], lo)
                across(wave, xs[nearest[i]], order[k], hi)

    got(recv1.at[0, pl.ds(0, 7)], came1.at[0])

    @pl.when(core == 0)
    def _():
        got(recv0.at[pl.ds(0, 7)], came0)

    unpack(0)
    first_leg(0)

    @pl.when(far_half == 0)
    def _():
        pl.semaphore_wait(far_sem, 8)
        for k in range(8):
            far_piece(k).start()
        for k in range(4):
            far_lead(k).start()

    second_leg(0)
    got(recv1.at[1], came1.at[1])

    @pl.when(core == 1)
    def _():
        got(recv0, came0)

    unpack(1)
    first_leg(1)

    second_leg(1)
    last_leg(0)
    last_leg(1)

    for wave in range(2):
        got(g_ref.at[wave, pl.ds(0, 16)], sib_sem.at[wave])

    def left(ref, send_sem):
        remote(ref, ref, send_sem, load_sem.at[0], (sib, c)).wait_send()

    for wave in range(2):
        left(g_ref.at[wave, pl.ds(0, 31)], sent.at[wave])
    left(send1.at[0, pl.ds(0, 7)], sent1.at[0])
    left(send1.at[1], sent1.at[1])
    left(recv0.at[pl.ds(0, 3)], sent0.at[0])
    left(recv0.at[pl.ds(0, 4)], sent0.at[1])
    pl.when(core == 1)(near_lead(0).wait_send)
    for load in loads[2:]:
        load.wait()


def early():
    r, c = lax.axis_index("row"), lax.axis_index("col")
    return jnp.logical_and(c < 4, 2 * (r // 8) + 2 * c + 3 * ((r // 2) % 4) <= EARLY)


def copy_kernel(q, z, q_out, z_out, held, in_sem, out_sem):
    @pl.when(early())
    def _():
        ins, outs = [], []
        for i in range(PARTS):
            part = pl.ds(128 // PARTS * i, 128 // PARTS)
            for n, (src, dst) in enumerate(((q, q_out), (z, z_out))):
                spot = 2 * i + n
                ins.append(pltpu.make_async_copy(src.at[part], held.at[n, part], in_sem.at[spot]))
                outs.append(pltpu.make_async_copy(held.at[n, part], dst.at[part], out_sem.at[spot]))
        for copy in ins:
            copy.start()
        for arrive, leave in zip(ins, outs):
            arrive.wait()
            leave.start()
        for copy in outs:
            copy.wait()


def apply_kernel(
    starts, flags, q, z, s, t, g, q_copied, z_copied, q_out, z_out, s_out, t_out, q_new, z_new, band, q_sem, z_sem, b_sem, whole_sem
):
    r = lax.axis_index("row")
    c = lax.axis_index("col")
    wholes = [pltpu.make_async_copy(q, q_out, whole_sem.at[0]), pltpu.make_async_copy(z, z_out, whole_sem.at[1])]
    for whole in wholes:
        pl.when(jnp.logical_not(early()))(whole.start)

    word = slot_words(starts, c)
    count = jnp.int32(0)
    windows = jnp.int32(0)
    for k in range(K):
        mine = (starts[k] >> 13) == c
        count = count + jnp.where(mine, 1, 0)
        bit = jnp.left_shift(jnp.int32(1), (starts[k] >> 8) & (TILES - 1))
        windows = jnp.where(jnp.logical_and(mine, flags[k] == 1), windows | bit, windows)

    def q_copy(j, tile):
        return pltpu.make_async_copy(q_new.at[j], q_out.at[:, pl.ds(pl.multiple_of(tile * W, W), W)], q_sem.at[j])

    def z_copy(j, tile):
        return pltpu.make_async_copy(z_new.at[j], z_out.at[:, pl.ds(pl.multiple_of(tile * W, W), W)], z_sem.at[j])

    far_half = c // 4

    def factor(side, slot):
        parts = [g[h ^ far_half, :, side, slot].reshape(W, W // 2) for h in range(2)]
        return jnp.concatenate(parts, axis=1)

    band_slot = jnp.int32(0)
    slots = []
    for j in range(SLOTS):
        k = (word >> (4 * j)) & 15
        tile = (starts[k] >> 8) & (TILES - 1)
        live = jnp.logical_and(j < count, flags[k] == 1)
        band_slot = jnp.where(jnp.logical_and(j < count, tile == r), j, band_slot)
        slots.append((live, tile))

        where = pl.ds(pl.multiple_of(tile * W, W), W)
        q_new[j] = jnp.dot(q[:, where], factor(0, j), preferred_element_type=F32).astype(BF)
        z_new[j] = jnp.dot(z[:, where], factor(1, j), preferred_element_type=F32).astype(BF)

        if j % 2 == 1:
            for jj in range(j - 1, j + 1):
                live, tile = slots[jj]

                @pl.when(jnp.logical_and(live, early()))
                def _():
                    q_copy(jj, tile).start()
                    z_copy(jj, tile).start()

    band_live = ((windows >> r) & 1) == 1
    right = factor(1, band_slot)
    lead = jnp.concatenate(
        [g[h ^ far_half, :, h ^ far_half, SLOTS].reshape(W, W // 2) for h in range(2)], axis=1
    )
    outs = []
    for i, (ref, out) in enumerate(((s, s_out), (t, t_out))):
        fresh = jnp.dot(ref[...], right, preferred_element_type=F32).astype(BF)
        mid = jnp.where(band_live, fresh, ref[...])
        band[i] = lax.dot_general(
            lead, mid, (((0,), (0,)), ((), ())), preferred_element_type=F32
        ).astype(BF)
        copy = pltpu.make_async_copy(band.at[i], out, b_sem.at[i])
        copy.start()
        outs.append(copy)
    for whole, new_copy in zip(wholes, (q_copy, z_copy)):
        pl.when(jnp.logical_not(early()))(whole.wait)
        for j, (live, tile) in enumerate(slots):
            pl.when(jnp.logical_and(live, jnp.logical_not(early())))(new_copy(j, tile).start)

    for copy in outs:
        copy.wait()
    for j, (live, tile) in enumerate(slots):

        @pl.when(live)
        def _():
            q_copy(j, tile).wait()
            z_copy(j, tile).wait()


def local(s_band, t_band, q_rows, z_rows, factors, starts, flags):
    anywhere = pl.BlockSpec(memory_space=pl.ANY)
    hbm = pl.BlockSpec(memory_space=pltpu.HBM)
    vmem = pl.BlockSpec(memory_space=pltpu.VMEM)
    smem = pl.BlockSpec(memory_space=pltpu.SMEM)
    dma = pltpu.SemaphoreType.DMA
    copied = pl.pallas_call(
        copy_kernel,
        out_shape=(
            jax.ShapeDtypeStruct(q_rows.shape, BF),
            jax.ShapeDtypeStruct(z_rows.shape, BF),
        ),
        in_specs=[hbm] * 2,
        out_specs=[hbm] * 2,
        scratch_shapes=[pltpu.VMEM((2, *q_rows.shape), BF), dma((2 * PARTS,)), dma((2 * PARTS,))],
        compiler_params=pltpu.CompilerParams(vmem_limit_bytes=32 << 20),
    )(*(pltpu.with_memory_space_constraint(a, pltpu.HBM) for a in (q_rows, z_rows)))
    gathered, qv, zv, sv, tv, starts_held, flags_held = pl.pallas_call(
        gather_kernel,
        out_shape=(
            pltpu.VMEM((2, ROWS, UNITS, 16, 128), BF),
            pltpu.VMEM(q_rows.shape, BF),
            pltpu.VMEM(z_rows.shape, BF),
            pltpu.VMEM(s_band.shape, BF),
            pltpu.VMEM(t_band.shape, BF),
            pltpu.SMEM((K,), jnp.int32),
            pltpu.SMEM((K,), jnp.int32),
        ),
        in_specs=[hbm] * 9,
        out_specs=[vmem] * 5 + [smem] * 2,
        scratch_shapes=[
            pltpu.VMEM((K, 2, 8, 32), BF),
            pltpu.VMEM((K, 16, 128), F32),
            pltpu.VMEM((2, 8, 16, 128), BF),
            pltpu.VMEM((2, 8, 16, 128), BF),
            pltpu.VMEM((16, 128), BF),
            pltpu.VMEM((8, 16, 128), BF),
            dma((7,)),
            dma((2,)), dma((3,)), dma((2,)), dma(()),
            dma((2,)), dma((2, 4)), dma((2, 4)), dma((2, 4)), dma((2,)),
            pltpu.SemaphoreType.REGULAR,
        ],
        compiler_params=pltpu.CompilerParams(
            collective_id=0, has_side_effects=True, vmem_limit_bytes=32 << 20
        ),
    )(*(pltpu.with_memory_space_constraint(a, pltpu.HBM) for a in (starts, flags, factors, q_rows, z_rows, s_band, t_band, *copied)))
    gathered = gathered.reshape(2, 16, 2, UNITS, 16, 128)
    pin = lambda a: pltpu.with_memory_space_constraint(a, pltpu.VMEM)
    return tuple(
        pl.pallas_call(
            apply_kernel,
            out_shape=(
                jax.ShapeDtypeStruct(q_rows.shape, BF),
                jax.ShapeDtypeStruct(z_rows.shape, BF),
                jax.ShapeDtypeStruct(s_band.shape, BF),
                jax.ShapeDtypeStruct(t_band.shape, BF),
            ),
            in_specs=[smem, smem] + [vmem] * 5 + [hbm] * 2,
            out_specs=[hbm] * 2 + [anywhere] * 2,
            input_output_aliases={7: 0, 8: 1},
            scratch_shapes=[
                pltpu.VMEM((SLOTS, 128, W), BF),
                pltpu.VMEM((SLOTS, 128, W), BF),
                pltpu.VMEM((2, W, W), BF),
                dma((SLOTS,)),
                dma((SLOTS,)),
                dma((2,)),
                dma((2,)),
            ],
            compiler_params=pltpu.CompilerParams(vmem_limit_bytes=32 << 20),
        )(*(pltpu.with_memory_space_constraint(a, pltpu.SMEM) for a in (starts_held, flags_held)), *(pin(a) for a in (qv, zv, sv, tv, gathered)), *(pltpu.with_memory_space_constraint(a, pltpu.HBM) for a in copied))
    )


def solution(mesh):
    in_specs = (
        P(None, ("col", "row")),
        P(None, ("col", "row")),
        P("row", "col"),
        P("row", "col"),
        P(None, None, "row", "col"),
        P(),
        P(),
    )
    out_specs = (P("row", "col"), P("row", "col"), P(None, ("col", "row")), P(None, ("col", "row")))
    return jax.shard_map(local, mesh=mesh, in_specs=in_specs, out_specs=out_specs, check_vma=False)
```
